128 devices in a mesh: dp: 4 (over z), ctx: 32 (over y, x, core).
Axes of the slice: x: 4, y: 4, z: 4, core: 2. Of those that a mesh axis runs over, the one named last changes fastest.
Arguments:
- streams: bfloat16 [32768, 12288], P(('dp', 'ctx')), parts along dimension 0, may hold values from -6 to 6
- short_filter: float32 [3, 12288], replicated, may hold values from -3 to 3
- rates: float32 [256, 16], replicated, may hold values from 6.1035156e-05 to 0.03
- residues: float32 [256, 16], replicated, may hold values from -3 to 3
- skip: float32 [4096], replicated, may hold values from -4 to 4
Outputs:
- gated: float32 [32768, 4096], P(('dp', 'ctx')), parts along dimension 0
The draws below stay inside these ranges and needn't reach their ends.
There are 4 independent parts, one for each index of `dp`. The reference program is written for one: setup_inputs(seed, part) draws one part's arguments, and reference() takes and returns one part's arrays. A program takes and returns all parts, laid end to end along the dimension named above; an argument that names none is the same for every part. Nothing has to cross between parts.
All inputs are finite; a program needn't handle non-finite values.
Results may differ from the reference program's by a relative error of at most 0.0003.
Values may be sent and summed in bfloat16 or wider, within the bound.
A program may use at most 320 MiB of HBM per device.

```python
import math
import jax
import jax.numpy as jnp

CH = 4096
GROUP = 16
ORDER = 16
KSHORT = 3
GROUPS = 256
SEQ = 8192


def shard_levels(rng, shape, cuts, low, top_value):
    factor_of, own = 1.0, jax.random.fold_in(rng, 6)
    for dim, parts in cuts:
        draws = jnp.exp(jax.random.uniform(jax.random.fold_in(own, dim), (parts,), jnp.float32, low / len(cuts), top_value / len(cuts)))
        factor_of = factor_of * jnp.repeat(draws, shape[dim] // parts).reshape([-1 if axis == dim else 1 for axis in range(len(shape))])
    return factor_of


def noise(rng, shape, deviation, most, shards=(), held_as=jnp.bfloat16):
    gain = shard_levels(rng, shape, shards, -0.22, 0.18) if shards else 1.0
    result = jax.random.normal(rng, shape, jnp.float32) * deviation * gain
    return jnp.minimum(jnp.maximum(result, -most), most).astype(held_as)


def setup_inputs(seed: int = 0, part: int = 0) -> dict:
    key_list = jax.random.split(jax.random.key(seed), 6)
    part_splits = jax.random.split(jax.random.fold_in(key_list[5], part), 6)
    streams = noise(part_splits[0], (SEQ, 3 * CH), 1.0, 6.0, ((0, 32),))
    short_filter = noise(key_list[1], (KSHORT, 3 * CH), 0.6, 3.0, (), jnp.float32)
    rates = jnp.clip(jnp.exp(jax.random.uniform(key_list[2], (GROUPS, ORDER), jnp.float32, math.log(6.103515625e-05), math.log(0.03))), 6.103515625e-05, 0.03)
    residues = noise(key_list[3], (GROUPS, ORDER), 0.5, 3.0, (), jnp.float32)
    skip = noise(key_list[4], (CH,), 1.0, 4.0, (), jnp.float32)
    return dict(streams=streams, short_filter=short_filter, rates=rates, residues=residues, skip=skip)


def reference(streams, short_filter, rates, residues, skip):
    zf = streams.astype(jnp.float32)
    width = KSHORT - 1
    zpad = jnp.concatenate([jnp.zeros((width, 3 * CH), jnp.float32), zf], axis=0)
    feat = jnp.zeros((SEQ, 3 * CH), jnp.float32)
    for tap in range(KSHORT):
        feat = feat + short_filter[tap][None, :] * zpad[width - tap:width - tap + SEQ]
    query = feat[:, :CH]
    key_part = feat[:, CH:2 * CH]
    value = feat[:, 2 * CH:]
    inner = key_part * value
    amp = residues * (-jnp.expm1(-rates))
    times = jnp.arange(SEQ).astype(jnp.float32)
    modes = jnp.exp(-times[:, None, None] * rates[None, :, :])
    filt = jnp.sum(modes * amp[None, :, :], axis=2)
    length = 2 * SEQ
    filt_spec = jnp.repeat(jnp.fft.rfft(filt, n=length, axis=0), GROUP, axis=1)
    spec = jnp.fft.rfft(inner, n=length, axis=0) * filt_spec
    conv = jnp.fft.irfft(spec, n=length, axis=0)[:SEQ].astype(jnp.float32)
    return query * (conv + skip[None, :] * inner)
```

```python
import functools

import jax
import jax.numpy as jnp
from jax import lax
from jax.experimental import pallas as pl
from jax.experimental.pallas import tpu as pltpu
from jax.sharding import PartitionSpec as P

F32 = jnp.float32
BF16 = jnp.bfloat16
LANES = 128
BLOCK = 16
SPAN = 2 * BLOCK
PER_CHUNK = 4
WIDE = PER_CHUNK * LANES


def halves(x):
    high = x.astype(BF16)
    return high, (x - high.astype(F32)).astype(BF16)


def group_mask():
    row = lax.broadcasted_iota(jnp.int32, (LANES, LANES), 0) // BLOCK
    lane = lax.broadcasted_iota(jnp.int32, (LANES, LANES), 1) // BLOCK
    return row == lane


def spread(mask, x):
    return jnp.where(mask, jnp.concatenate([x] * (LANES // BLOCK), axis=0), jnp.zeros((), BF16))


def paired(mask, first, second):
    first, second = halves(first), halves(second)
    left = jnp.concatenate([spread(mask, first[0]), spread(mask, first[1])], axis=0)
    right = jnp.concatenate([spread(mask, second[0]), spread(mask, second[1])], axis=0)
    return jnp.concatenate([left, right], axis=1)


def stack_rows(parts):
    rows = []
    for part, is_low in parts:
        other = jnp.zeros_like(part) if is_low else part
        rows.append(jnp.concatenate([part, other], axis=1))
    return jnp.concatenate(rows, axis=0)


def main_kernel(
    count, streams, taps, rate, amp, skip,
    loc, query, local_states, decay, forward, incoming,
    xs, last, rim_out, rim_in, weights, shifted, sums_out, sums_in, back_out, back_in,
    stream_sem, last_sem, rim_sems, sums_send, sums_recv, back_send, back_recv,
):
    rows = loc.shape[0]
    channels = loc.shape[1]
    tiles = channels // LANES
    chunks = tiles // PER_CHUNK
    blocks = rows // BLOCK
    me = lax.axis_index("ctx")

    def stream_copy(s, c):
        return pltpu.make_async_copy(
            streams.at[:, pl.ds(pl.multiple_of(s * channels + c * WIDE, WIDE), WIDE)],
            xs.at[s, c], stream_sem.at[s, c])

    def chunk_at(k):
        return lax.rem(me // PER_CHUNK + 1 + k, chunks)

    last_copy = pltpu.make_async_copy(streams.at[pl.ds(rows - BLOCK, BLOCK), :], last, last_sem)
    last_copy.start()

    @pl.loop(0, chunks)
    def _(k):
        c = chunk_at(k)
        stream_copy(1, c).start()
        stream_copy(2, c).start()

    barrier = pltpu.get_barrier_semaphore()

    @pl.loop(1, count)
    def _(i):
        pl.semaphore_signal(barrier, inc=1, device_id={"ctx": lax.rem(me + i, count)},
                            device_id_type=pl.DeviceIdType.MESH)

    last_copy.wait()

    @pl.loop(0, 3 * chunks)
    def _(e):
        for p in range(PER_CHUNK):
            lane = pl.ds(pl.multiple_of(e * WIDE + p * LANES, LANES), LANES)
            rim_out[e, 2 * p:2 * p + 2, :] = last[:, lane].astype(F32)[BLOCK - 2:]

    pl.semaphore_wait(barrier, count - 1)
    rim_copy = pltpu.make_async_remote_copy(
        src_ref=rim_out, dst_ref=rim_in, send_sem=rim_sems.at[0], recv_sem=rim_sems.at[1],
        device_id={"ctx": lax.rem(me + 1, count)}, device_id_type=pl.DeviceIdType.MESH)
    rim_copy.start()

    @pl.loop(0, chunks)
    def _(k):
        stream_copy(0, chunk_at(k)).start()

    @pl.loop(0, tiles)
    def _(t):
        lane = pl.ds(pl.multiple_of(t * LANES, LANES), LANES)
        r = rate[:, lane]
        a = amp[:, lane]
        inside = lax.broadcasted_iota(jnp.int32, (BLOCK, LANES), 1) % BLOCK
        row = lax.broadcasted_iota(jnp.int32, (BLOCK, LANES), 0)
        gap = (row - inside).astype(F32)
        near = jnp.zeros((BLOCK, LANES), F32)
        far = jnp.zeros((BLOCK, LANES), F32)
        step = jnp.exp(-float(BLOCK) * r)
        for n in range(BLOCK):
            one = a[n:n + 1] * jnp.exp(-r[n:n + 1] * gap)
            near = near + one
            far = far + one * step[n:n + 1]
        near = halves(jnp.where(row >= inside, near, 0.0))
        far = halves(far)
        back = halves(jnp.exp(-r * (BLOCK - 1.0 - inside.astype(F32))))
        weights[t] = stack_rows([(far[0], False), (far[1], True), (near[0], False), (back[0], False),
                                 (near[1], True), (back[1], True)])
        decay[:, lane] = jnp.exp(-float(SPAN) * r)
        own = row == inside
        r_own = jnp.sum(jnp.where(own, r, 0.0), axis=0, keepdims=True)
        a_own = jnp.sum(jnp.where(own, a, 0.0), axis=0, keepdims=True)
        out = lax.broadcasted_iota(jnp.int32, (SPAN, LANES), 0).astype(F32) + 1.0
        out = halves(a_own * jnp.exp(-r_own * out))
        forward[t] = stack_rows([(out[0], False), (out[1], True)])

    rim_copy.wait()
    first = jnp.where(me > 0, 1.0, 0.0)

    def shifted_rows(slot, s, c, j):
        lane = pl.ds(pl.multiple_of(j * LANES, LANES), LANES)
        shifted[slot, pl.ds(6, 2), :] = rim_in[s * chunks + c, pl.ds(2 * j, 2), :] * first
        for b in range(blocks):
            shifted[slot, pl.ds(8 + BLOCK * b, BLOCK), :] = xs[s, c, pl.ds(BLOCK * b, BLOCK), lane].astype(F32)

    def filtered(slot, s, t, b):
        lane = pl.ds(pl.multiple_of(s * channels + t * LANES, LANES), LANES)
        total = taps[0:1, lane] * shifted[slot, pl.ds(8 + BLOCK * b, BLOCK), :]
        for tap in (1, 2):
            total = total + taps[tap:tap + 1, lane] * shifted[slot, pl.ds(8 + BLOCK * b - tap, BLOCK), :]
        return total

    def sums_copy(t):
        return pltpu.make_async_remote_copy(
            src_ref=sums_out.at[t], dst_ref=sums_in.at[me], send_sem=sums_send.at[t], recv_sem=sums_recv.at[me],
            device_id={"ctx": t}, device_id_type=pl.DeviceIdType.MESH)

    mask = group_mask()

    @pl.loop(0, chunks)
    def _(k):
        c = chunk_at(k)
        stream_copy(1, c).wait()
        stream_copy(2, c).wait()

        @pl.loop(0, PER_CHUNK)
        def _(i):
            j = lax.rem(me + 1 + i, PER_CHUNK)
            t = c * PER_CHUNK + j
            lane = pl.ds(pl.multiple_of(t * LANES, LANES), LANES)
            shifted_rows(0, 1, c, j)
            shifted_rows(1, 2, c, j)
            step = jnp.exp(-float(BLOCK) * rate[:, lane])
            direct = skip[0:1, lane]
            state = jnp.zeros((BLOCK, LANES), F32)
            for quad in range(blocks // 4):
                inner = [filtered(0, 1, t, 4 * quad + b) * filtered(1, 2, t, 4 * quad + b) for b in range(4)]
                even = jnp.dot(weights[t], paired(mask, inner[0], inner[2]), preferred_element_type=F32)
                odd = jnp.dot(weights[t, 2 * BLOCK:, :], paired(mask, inner[1], inner[3]), preferred_element_type=F32)
                for b in range(4):
                    side = slice((b // 2) * LANES, (b // 2 + 1) * LANES)
                    part = odd[:, side] if b % 2 else even[2 * BLOCK:, side]
                    value = direct * inner[b] + (part[:BLOCK] + part[2 * BLOCK:3 * BLOCK])
                    if b % 2:
                        value = value + (even[:BLOCK, side] + even[BLOCK:2 * BLOCK, side])
                    else:
                        local_states[(4 * quad + b) // 2, :, lane] = state
                    loc[pl.ds((4 * quad + b) * BLOCK, BLOCK), lane] = value
                    state = state * step + (part[BLOCK:2 * BLOCK] + part[3 * BLOCK:])

            @pl.when(t != me)
            def _():
                sums_out[t] = state
                sums_copy(t).start()

            @pl.when(t == me)
            def _():
                sums_in[me] = state

    @pl.loop(0, chunks)
    def _(k):
        c = chunk_at(k)
        stream_copy(0, c).wait()

        @pl.loop(0, PER_CHUNK)
        def _(j):
            t = c * PER_CHUNK + j
            lane = pl.ds(pl.multiple_of(t * LANES, LANES), LANES)
            shifted_rows(0, 0, c, j)
            for b in range(blocks):
                query[pl.ds(b * BLOCK, BLOCK), lane] = filtered(0, 0, t, b)

    def sums_arrival(d):
        return pltpu.make_async_remote_copy(
            src_ref=sums_out.at[d], dst_ref=sums_in.at[d], send_sem=sums_send.at[d], recv_sem=sums_recv.at[d],
            device_id={"ctx": d}, device_id_type=pl.DeviceIdType.MESH)

    def back_copy(d):
        return pltpu.make_async_remote_copy(
            src_ref=back_out.at[d], dst_ref=back_in.at[me], send_sem=back_send.at[d], recv_sem=back_recv.at[me],
            device_id={"ctx": d}, device_id_type=pl.DeviceIdType.MESH)

    def back_arrival(d):
        return pltpu.make_async_remote_copy(
            src_ref=back_out.at[d], dst_ref=back_in.at[d], send_sem=back_send.at[d], recv_sem=back_recv.at[d],
            device_id={"ctx": d}, device_id_type=pl.DeviceIdType.MESH)

    own_lane = pl.ds(pl.multiple_of(me * LANES, LANES), LANES)
    device_decay = jnp.exp(-float(rows) * rate[:, own_lane])

    def turn(d, before):
        @pl.when(d != me)
        def _():
            sums_arrival(d).wait_recv()
            back_out[d] = before
            back_copy(d).start()

        @pl.when(d == me)
        def _():
            back_in[me] = before

        return before * device_decay + sums_in[d]

    lax.fori_loop(0, count, turn, jnp.zeros((BLOCK, LANES), F32))

    @pl.loop(1, count)
    def _(i):
        d = lax.rem(me + i, count)
        back_arrival(d).wait_recv()
        sums_arrival(d).wait_send()
        back_copy(d).wait_send()

    for t in range(tiles):
        incoming[:, t * LANES:(t + 1) * LANES] = back_in[t]


def last_kernel(loc, query, local_states, decay, forward, incoming, out):
    step = pl.program_id(0)
    wide = out.shape[1]
    rows = out.shape[0]
    mask = group_mask()

    @pl.loop(0, wide // LANES)
    def _(j):
        t = step * (wide // LANES) + j
        lane = pl.ds(pl.multiple_of(t * LANES, LANES), LANES)
        here = pl.ds(pl.multiple_of(j * LANES, LANES), LANES)
        carried = incoming[:, lane]
        fade = decay[:, lane]
        for pair in range(rows // SPAN // 2):
            states = []
            for m in (2 * pair, 2 * pair + 1):
                states.append(local_states[m, :, lane] + carried)
                carried = carried * fade
            both = jnp.dot(forward[t], paired(mask, *states), preferred_element_type=F32)
            for side in range(2):
                at = pl.ds((2 * pair + side) * SPAN, SPAN)
                value = both[:, side * LANES:(side + 1) * LANES]
                out[at, here] = query[at, lane] * (loc[at, lane] + (value[:SPAN] + value[SPAN:]))


def body(count, streams, short_filter, rates, residues, skip):
    rows = streams.shape[0]
    channels = skip.shape[0]
    tiles = channels // LANES
    chunks = tiles // PER_CHUNK
    rate = jnp.repeat(rates.T, BLOCK, axis=1)
    amp = jnp.repeat((residues * -jnp.expm1(-rates)).T, BLOCK, axis=1)
    vmem = pl.BlockSpec(memory_space=pltpu.VMEM)
    shapes = (
        ((rows, channels), F32),
        ((rows, channels), F32),
        ((rows // SPAN, BLOCK, channels), F32),
        ((BLOCK, channels), F32),
        ((tiles, 2 * SPAN, 2 * LANES), BF16),
        ((BLOCK, channels), F32),
    )
    parts = pl.pallas_call(
        functools.partial(main_kernel, count),
        out_shape=tuple(pltpu.VMEM(shape, dtype) for shape, dtype in shapes),
        in_specs=[pl.BlockSpec(memory_space=pl.ANY)] + [vmem] * 4,
        out_specs=(vmem,) * len(shapes),
        scratch_shapes=[
            pltpu.VMEM((3, chunks, rows, WIDE), BF16),
            pltpu.VMEM((BLOCK, 3 * channels), BF16),
            pltpu.VMEM((3 * chunks, 8, LANES), F32),
            pltpu.VMEM((3 * chunks, 8, LANES), F32),
            pltpu.VMEM((tiles, 6 * BLOCK, 2 * LANES), BF16),
            pltpu.VMEM((2, rows + 8, LANES), F32),
            pltpu.VMEM((count, BLOCK, LANES), F32),
            pltpu.VMEM((count, BLOCK, LANES), F32),
            pltpu.VMEM((count, BLOCK, LANES), F32),
            pltpu.VMEM((count, BLOCK, LANES), F32),
            pltpu.SemaphoreType.DMA((3, chunks)),
            pltpu.SemaphoreType.DMA,
            pltpu.SemaphoreType.DMA((2,)),
            pltpu.SemaphoreType.DMA((count,)),
            pltpu.SemaphoreType.DMA((count,)),
            pltpu.SemaphoreType.DMA((count,)),
            pltpu.SemaphoreType.DMA((count,)),
        ],
        compiler_params=pltpu.CompilerParams(
            collective_id=0, has_side_effects=True, vmem_limit_bytes=24 << 20),
        name="local_part",
    )(streams, short_filter, rate, amp, skip[None, :])
    parts = [pltpu.with_memory_space_constraint(part, pltpu.VMEM) for part in parts]
    return pl.pallas_call(
        last_kernel,
        grid=(chunks,),
        out_shape=jax.ShapeDtypeStruct((rows, channels), F32),
        in_specs=[vmem] * len(parts),
        out_specs=pl.BlockSpec((rows, WIDE), lambda i: (0, i)),
        compiler_params=pltpu.CompilerParams(vmem_limit_bytes=12 << 20),
        name="carried_part",
    )(*parts)


def solution(mesh):
    count = mesh.shape["ctx"]
    in_specs = (P(("dp", "ctx"), None), P(), P(), P(), P())
    out_specs = P(("dp", "ctx"), None)
    return jax.shard_map(functools.partial(body, count), mesh=mesh, in_specs=in_specs, out_specs=out_specs,
                         check_vma=False)
```

```python
import functools

import jax
import jax.numpy as jnp
from jax import lax
from jax.experimental import pallas as pl
from jax.experimental.pallas import tpu as pltpu
from jax.sharding import PartitionSpec as P

F32 = jnp.float32
BF16 = jnp.bfloat16
LANES = 128
BLOCK = 16
SPAN = 2 * BLOCK
PER_CHUNK = 4
WIDE = PER_CHUNK * LANES
EDGES = 8
UNROLL = 2
MESH = pl.DeviceIdType.MESH


def halves(x):
    high = x.astype(BF16)
    return high, (x - high.astype(F32)).astype(BF16)


def group_mask(lanes):
    row = lax.broadcasted_iota(jnp.int32, (lanes, lanes), 0) // BLOCK
    lane = lax.broadcasted_iota(jnp.int32, (lanes, lanes), 1) // BLOCK
    return row == lane


def spread(mask, x):
    return jnp.where(mask, jnp.concatenate([x] * (mask.shape[0] // BLOCK), axis=0), jnp.zeros((), BF16))


def paired(mask, first, second):
    first, second = halves(first), halves(second)
    left = jnp.concatenate([spread(mask, first[0]), spread(mask, first[1])], axis=0)
    right = jnp.concatenate([spread(mask, second[0]), spread(mask, second[1])], axis=0)
    return jnp.concatenate([left, right], axis=1)


def stack_rows(parts):
    rows = []
    for part, is_low in parts:
        other = jnp.zeros_like(part) if is_low else part
        rows.append(jnp.concatenate([part, other], axis=1))
    return jnp.concatenate(rows, axis=0)


def rim_effect(key_taps, value_taps, edge, rim):
    k0, k1, v0, v1 = edge
    kb, ka, vb, va = rim
    base_k, base_v = key_taps[0] * k0, value_taps[0] * v0
    more_k, more_v = key_taps[1] * ka + key_taps[2] * kb, value_taps[1] * va + value_taps[2] * vb
    first = more_k * base_v + (base_k + more_k) * more_v
    base_k, base_v = key_taps[0] * k1 + key_taps[1] * k0, value_taps[0] * v1 + value_taps[1] * v0
    more_k, more_v = key_taps[2] * ka, value_taps[2] * va
    second = more_k * base_v + (base_k + more_k) * more_v
    return first, second


def main_kernel(
    count, streams, taps_in, rates, residues, skip_in,
    loc, query, forward_high, forward_low, incoming,
    xs, last, taps, skip, few_rates, few_residues, rate, amp, local_states,
    rim_out, rim_in, weights, shifted, sums_out, sums_in, back_out, back_in,
    stream_sem, small_sem, rim_sems, sums_send, sums_recv, back_send, back_recv,
):
    rows, channels = loc.shape
    tiles = channels // LANES
    chunks = tiles // PER_CHUNK
    blocks = rows // BLOCK
    me = lax.axis_index("ctx")

    def stream_copy(s, c):
        return pltpu.make_async_copy(
            streams.at[:, pl.ds(pl.multiple_of(s * channels + c * WIDE, WIDE), WIDE)],
            xs.at[s, c], stream_sem.at[s, c])

    def chunk_at(k):
        return lax.rem(me // PER_CHUNK + 1 + k, chunks)

    small = [pltpu.make_async_copy(a, b, small_sem.at[i]) for i, (a, b) in enumerate((
        (rates, few_rates), (residues, few_residues), (taps_in, taps), (skip_in, skip),
        (streams.at[pl.ds(rows - BLOCK, BLOCK), :], last)))]
    for copy in small:
        copy.start()

    @pl.loop(0, chunks)
    def _(k):
        c = chunk_at(k)
        stream_copy(1, c).start()
        stream_copy(2, c).start()

    barrier = pltpu.get_barrier_semaphore()

    @pl.loop(1, count)
    def _(i):
        pl.semaphore_signal(barrier, inc=1, device_id={"ctx": lax.rem(me + i, count)}, device_id_type=MESH)

    @pl.loop(0, chunks)
    def _(k):
        stream_copy(0, chunk_at(k)).start()

    small[0].wait()
    small[1].wait()
    few = few_rates[...]
    few_residues[...] = few_residues[...] * (few * (1.0 - few / 2 * (1.0 - few / 3 * (1.0 - few / 4 * (
        1.0 - few / 5 * (1.0 - few / 6))))))

    @pl.loop(0, tiles)
    def _(t):
        lane = pl.ds(pl.multiple_of(t * LANES, LANES), LANES)
        inside = lax.broadcasted_iota(jnp.int32, (BLOCK, LANES), 1) % BLOCK
        row = lax.broadcasted_iota(jnp.int32, (BLOCK, LANES), 0)
        group = t * (LANES // BLOCK)
        part = pl.ds(pl.multiple_of(group // LANES * LANES, LANES), LANES)
        pick = lax.broadcasted_iota(jnp.int32, (BLOCK, LANES), 1) // BLOCK + lax.rem(group, LANES)
        r = jnp.take_along_axis(few_rates[:, part], pick, axis=1, mode="promise_in_bounds")
        a = jnp.take_along_axis(few_residues[:, part], pick, axis=1, mode="promise_in_bounds")
        rate[:, lane] = r
        amp[:, lane] = a
        gap = (row - inside).astype(F32)
        near = jnp.zeros((BLOCK, LANES), F32)
        far = jnp.zeros((BLOCK, LANES), F32)
        step = jnp.exp(-float(BLOCK) * r)
        for n in range(BLOCK):
            one = a[n:n + 1] * jnp.exp(-r[n:n + 1] * gap)
            near = near + one
            far = far + one * step[n:n + 1]
        near = halves(jnp.where(row >= inside, near, 0.0))
        far = halves(far)
        back = halves(jnp.exp(-r * (BLOCK - 1.0 - inside.astype(F32))))
        weights[t] = stack_rows([(far[0], False), (far[1], True), (near[0], False), (back[0], False),
                                 (near[1], True), (back[1], True)])

    for copy in small[2:]:
        copy.wait()

    rim_copy = pltpu.make_async_remote_copy(
        src_ref=rim_out, dst_ref=rim_in, send_sem=rim_sems.at[0], recv_sem=rim_sems.at[1],
        device_id={"ctx": lax.rem(me + 1, count)}, device_id_type=MESH)

    def shifted_rows(slot, s, c, j, rim):
        lane = pl.ds(pl.multiple_of(j * LANES, LANES), LANES)
        shifted[slot, pl.ds(6, 2), :] = rim
        for b in range(blocks):
            shifted[slot, pl.ds(8 + BLOCK * b, BLOCK), :] = xs[s, c, pl.ds(BLOCK * b, BLOCK), lane].astype(F32)

    def stream_taps(s, t):
        lane = pl.ds(pl.multiple_of(s * channels + t * LANES, LANES), LANES)
        return [taps[tap:tap + 1, lane] for tap in range(3)]

    def filtered(slot, by, b):
        total = by[0] * shifted[slot, pl.ds(8 + BLOCK * b, BLOCK), :]
        for tap in (1, 2):
            total = total + by[tap] * shifted[slot, pl.ds(8 + BLOCK * b - tap, BLOCK), :]
        return total

    def sums_copy(t):
        return pltpu.make_async_remote_copy(
            src_ref=sums_out.at[t], dst_ref=sums_in.at[me], send_sem=sums_send.at[t], recv_sem=sums_recv.at[me],
            device_id={"ctx": t}, device_id_type=MESH)

    def tile_at(k, i):
        c = chunk_at(k)
        j = lax.rem(me + 1 + i, PER_CHUNK)
        return c, j, c * PER_CHUNK + j

    mask = group_mask(LANES)
    greeted = chunks // 2
    nothing = jnp.zeros((2, LANES), F32)

    def local_tile(u, k, i):
        c, j, t = tile_at(k, i)
        lane = pl.ds(pl.multiple_of(t * LANES, LANES), LANES)
        at_key, at_value = 2 * u, 2 * u + 1
        shifted_rows(at_key, 1, c, j, nothing)
        shifted_rows(at_value, 2, c, j, nothing)
        by_key, by_value = stream_taps(1, t), stream_taps(2, t)
        step = jnp.exp(-float(BLOCK) * rate[:, lane])
        direct = skip[0:1, lane]
        state = jnp.zeros((BLOCK, LANES), F32)
        for quad in range(blocks // 4):
            inner = [filtered(at_key, by_key, 4 * quad + b) * filtered(at_value, by_value, 4 * quad + b)
                     for b in range(4)]
            even = jnp.dot(weights[t], paired(mask, inner[0], inner[2]), preferred_element_type=F32)
            odd = jnp.dot(weights[t, 2 * BLOCK:, :], paired(mask, inner[1], inner[3]), preferred_element_type=F32)
            for b in range(4):
                side = slice((b // 2) * LANES, (b // 2 + 1) * LANES)
                part = odd[:, side] if b % 2 else even[2 * BLOCK:, side]
                value = direct * inner[b] + (part[:BLOCK] + part[2 * BLOCK:3 * BLOCK])
                if b % 2:
                    value = value + (even[:BLOCK, side] + even[BLOCK:2 * BLOCK, side])
                else:
                    local_states[t, (4 * quad + b) // 2] = state
                loc[pl.ds((4 * quad + b) * BLOCK, BLOCK), lane] = value
                state = state * step + (part[BLOCK:2 * BLOCK] + part[3 * BLOCK:])
        sums_out[t, 0:BLOCK] = state
        end = 6 + rows
        sums_out[t, pl.ds(BLOCK, 2)] = shifted[at_key, pl.ds(8, 2), :]
        sums_out[t, pl.ds(BLOCK + 2, 2)] = shifted[at_value, pl.ds(8, 2), :]
        sums_out[t, pl.ds(BLOCK + 4, 2)] = shifted[at_key, pl.ds(end, 2), :]
        sums_out[t, pl.ds(BLOCK + 6, 2)] = shifted[at_value, pl.ds(end, 2), :]

    def local_chunk(k):
        c = chunk_at(k)
        stream_copy(1, c).wait()
        stream_copy(2, c).wait()

        @pl.loop(0, PER_CHUNK, step=UNROLL)
        def _(i):
            for u in range(UNROLL):
                local_tile(u, k, i + u)

    def send_chunk(k):
        for i in range(PER_CHUNK):
            t = tile_at(k, i)[2]

            @pl.when(t != me)
            def _():
                sums_copy(t).start()

    @pl.loop(0, greeted)
    def _(k):
        local_chunk(k)

    @pl.loop(0, 3 * chunks)
    def _(e):
        for p in range(PER_CHUNK):
            lane = pl.ds(pl.multiple_of(e * WIDE + p * LANES, LANES), LANES)
            rim_out[e, 2 * p:2 * p + 2, :] = last[:, lane].astype(F32)[BLOCK - 2:]

    pl.semaphore_wait(barrier, count - 1)
    rim_copy.start()

    @pl.loop(0, greeted)
    def _(k):
        send_chunk(k)

    @pl.loop(greeted, chunks)
    def _(k):
        local_chunk(k)
        send_chunk(k)

    sums_in[me] = sums_out[me]
    rim_copy.wait()
    has_rim = jnp.where(me > 0, 1.0, 0.0)

    def rest_tile(k, j):
        c = chunk_at(k)
        t = c * PER_CHUNK + j
        lane = pl.ds(pl.multiple_of(t * LANES, LANES), LANES)
        r, a = rate[:, lane], amp[:, lane]
        inside = lax.broadcasted_iota(jnp.int32, (BLOCK, LANES), 1) % BLOCK
        row = lax.broadcasted_iota(jnp.int32, (BLOCK, LANES), 0)
        own = row == inside
        r_own = jnp.sum(jnp.where(own, r, 0.0), axis=0, keepdims=True)
        a_own = jnp.sum(jnp.where(own, a, 0.0), axis=0, keepdims=True)
        out = a_own * jnp.exp(-r_own * (row.astype(F32) + 1.0))
        step = jnp.exp(-float(BLOCK) * r_own)
        near = []
        for b in range(blocks):
            high, low = halves(out)
            forward_high[pl.ds(b * BLOCK, BLOCK), lane] = high
            forward_low[pl.ds(b * BLOCK, BLOCK), lane] = low
            if b < 2:
                near.append((high, low))
            out = out * step
        by = stack_rows([(near[0][0], False), (near[1][0], False), (near[0][1], True), (near[1][1], True)])
        rim = [rim_in[s * chunks + c, pl.ds(2 * j, 2), :] * has_rim for s in range(3)]
        edge = sums_out[t, pl.ds(BLOCK, 4)]
        first, second = rim_effect(
            stream_taps(1, t), stream_taps(2, t), [edge[i:i + 1] for i in range(4)],
            [rim[1][0:1], rim[1][1:2], rim[2][0:1], rim[2][1:2]])
        before = jnp.sum(a * jnp.exp(r), axis=0, keepdims=True)
        direct = skip[0:1, lane]
        loc[0:1, lane] += direct * first - before * second
        loc[1:2, lane] += direct * second

        shifted_rows(0, 0, c, j, rim[0])
        by_query = stream_taps(0, t)
        spans = rows // SPAN
        for pair in range(spans // 2):
            both = jnp.dot(by, paired(mask, local_states[t, 2 * pair], local_states[t, 2 * pair + 1]),
                           preferred_element_type=F32)
            for side in range(2):
                value = both[:, side * LANES:(side + 1) * LANES]
                for half in range(2):
                    b = (2 * pair + side) * 2 + half
                    at = pl.ds(b * BLOCK, BLOCK)
                    gate = filtered(0, by_query, b)
                    query[at, lane] = gate
                    loc[at, lane] = gate * (loc[at, lane] + (
                        value[half * BLOCK:(half + 1) * BLOCK] + value[SPAN + half * BLOCK:SPAN + (half + 1) * BLOCK]))

    def rest_chunk(k):
        stream_copy(0, chunk_at(k)).wait()

        @pl.loop(0, PER_CHUNK)
        def _(j):
            rest_tile(k, j)

    answered = chunks // 2

    @pl.loop(0, answered)
    def _(k):
        rest_chunk(k)

    def sums_arrival(d):
        return pltpu.make_async_remote_copy(
            src_ref=sums_out.at[d], dst_ref=sums_in.at[d], send_sem=sums_send.at[d], recv_sem=sums_recv.at[d],
            device_id={"ctx": d}, device_id_type=MESH)

    def back_copy(d):
        return pltpu.make_async_remote_copy(
            src_ref=back_out.at[d], dst_ref=back_in.at[me], send_sem=back_send.at[d], recv_sem=back_recv.at[me],
            device_id={"ctx": d}, device_id_type=MESH)

    def back_arrival(d):
        return pltpu.make_async_remote_copy(
            src_ref=back_out.at[d], dst_ref=back_in.at[d], send_sem=back_send.at[d], recv_sem=back_recv.at[d],
            device_id={"ctx": d}, device_id_type=MESH)

    @pl.loop(1, count)
    def _(i):
        sums_arrival(lax.rem(me + i, count)).wait_recv()

    r = rate[:, pl.ds(pl.multiple_of(me * LANES, LANES), LANES)]
    device_decay = jnp.exp(-float(rows) * r)
    ahead = jnp.exp(r)
    further = ahead * ahead
    key_taps, value_taps = stream_taps(1, me), stream_taps(2, me)
    state = jnp.zeros((BLOCK, LANES), F32)
    for d in range(count):
        if d:
            edge = sums_in[d, BLOCK:BLOCK + EDGES]
            rim = sums_in[d - 1, BLOCK:BLOCK + EDGES]
            first, second = rim_effect(key_taps, value_taps, [edge[i:i + 1] for i in range(4)],
                                       [rim[i:i + 1] for i in range(4, 8)])
            state = state + (ahead * first + further * second)
        back_out[d] = state
        state = state * device_decay + sums_in[d, 0:BLOCK]
    back_in[me] = back_out[me]

    @pl.loop(1, count)
    def _(i):
        back_copy(lax.rem(me + i, count)).start()

    @pl.loop(answered, chunks)
    def _(k):
        rest_chunk(k)

    @pl.loop(1, count)
    def _(i):
        d = lax.rem(me + i, count)
        back_arrival(d).wait_recv()
        sums_arrival(d).wait_send()
        back_copy(d).wait_send()

    for t in range(tiles):
        incoming[:, t * LANES:(t + 1) * LANES] = back_in[t]


def last_kernel(loc, query, forward_high, forward_low, incoming, out):
    step = pl.program_id(0)
    wide = out.shape[1]
    lanes = 2 * LANES
    mask = group_mask(lanes)
    for j in range(wide // lanes):
        lane = pl.ds(pl.multiple_of(step * wide + j * lanes, lanes), lanes)
        high, low = halves(incoming[:, lane])
        high, low = spread(mask, high), spread(mask, low)
        by_high, by_low = forward_high[:, lane], forward_low[:, lane]
        value = jnp.dot(jnp.concatenate([by_high, by_low, by_high], axis=1),
                        jnp.concatenate([high, high, low], axis=0), preferred_element_type=F32)
        out[:, j * lanes:(j + 1) * lanes] = loc[:, lane] + query[:, lane] * value


def body(count, streams, short_filter, rates, residues, skip):
    rows = streams.shape[0]
    channels = skip.shape[0]
    groups = rates.shape[0]
    tiles = channels // LANES
    chunks = tiles // PER_CHUNK
    vmem = pl.BlockSpec(memory_space=pltpu.VMEM)
    hbm = pl.BlockSpec(memory_space=pltpu.HBM)
    shapes = (
        ((rows, channels), F32),
        ((rows, channels), F32),
        ((rows, channels), BF16),
        ((rows, channels), BF16),
        ((BLOCK, channels), F32),
    )
    operands = (streams, short_filter, rates.T, residues.T, skip[None, :])
    operands = [pltpu.with_memory_space_constraint(x, pltpu.HBM) for x in operands]
    parts = pl.pallas_call(
        functools.partial(main_kernel, count),
        out_shape=tuple(pltpu.VMEM(shape, dtype) for shape, dtype in shapes),
        in_specs=[hbm] * 5,
        out_specs=(vmem,) * len(shapes),
        scratch_shapes=[
            pltpu.VMEM((3, chunks, rows, WIDE), BF16),
            pltpu.VMEM((BLOCK, 3 * channels), BF16),
            pltpu.VMEM(short_filter.shape, F32),
            pltpu.VMEM((1, channels), F32),
            pltpu.VMEM((BLOCK, groups), F32),
            pltpu.VMEM((BLOCK, groups), F32),
            pltpu.VMEM((BLOCK, channels), F32),
            pltpu.VMEM((BLOCK, channels), F32),
            pltpu.VMEM((tiles, rows // SPAN, BLOCK, LANES), F32),
            pltpu.VMEM((3 * chunks, 8, LANES), F32),
            pltpu.VMEM((3 * chunks, 8, LANES), F32),
            pltpu.VMEM((tiles, 6 * BLOCK, 2 * LANES), BF16),
            pltpu.VMEM((2 * UNROLL, rows + 8, LANES), F32),
            pltpu.VMEM((count, BLOCK + EDGES, LANES), F32),
            pltpu.VMEM((count, BLOCK + EDGES, LANES), F32),
            pltpu.VMEM((count, BLOCK, LANES), F32),
            pltpu.VMEM((count, BLOCK, LANES), F32),
            pltpu.SemaphoreType.DMA((3, chunks)),
            pltpu.SemaphoreType.DMA((5,)),
            pltpu.SemaphoreType.DMA((2,)),
            pltpu.SemaphoreType.DMA((count,)),
            pltpu.SemaphoreType.DMA((count,)),
            pltpu.SemaphoreType.DMA((count,)),
            pltpu.SemaphoreType.DMA((count,)),
        ],
        compiler_params=pltpu.CompilerParams(
            collective_id=0, has_side_effects=True, vmem_limit_bytes=24 << 20),
        name="local_part",
    )(*operands)
    parts = [pltpu.with_memory_space_constraint(part, pltpu.VMEM) for part in parts]
    return pl.pallas_call(
        last_kernel,
        grid=(chunks,),
        out_shape=jax.ShapeDtypeStruct((rows, channels), F32),
        in_specs=[vmem] * len(parts),
        out_specs=pl.BlockSpec((rows, WIDE), lambda i: (0, i)),
        compiler_params=pltpu.CompilerParams(vmem_limit_bytes=12 << 20),
        name="carried_part",
    )(*parts)


def solution(mesh):
    count = mesh.shape["ctx"]
    in_specs = (P(("dp", "ctx"), None), P(), P(), P(), P())
    out_specs = P(("dp", "ctx"), None)
    return jax.shard_map(functools.partial(body, count), mesh=mesh, in_specs=in_specs, out_specs=out_specs,
                         check_vma=False)
```

```python
import functools

import jax
import jax.numpy as jnp
from jax import lax
from jax.experimental import pallas as pl
from jax.experimental.pallas import tpu as pltpu
from jax.sharding import PartitionSpec as P

F32 = jnp.float32
BF16 = jnp.bfloat16
LANES = 128
BLOCK = 16
SPAN = 2 * BLOCK
PER_CHUNK = 4
WIDE = PER_CHUNK * LANES
EDGES = 8
PAIR = 2 * LANES
UNROLL = 2
MESH = pl.DeviceIdType.MESH


def halves(x):
    high = x.astype(BF16)
    return high, (x - high.astype(F32)).astype(BF16)


def group_mask(lanes):
    row = lax.broadcasted_iota(jnp.int32, (lanes, lanes), 0) // BLOCK
    lane = lax.broadcasted_iota(jnp.int32, (lanes, lanes), 1) // BLOCK
    return row == lane


def spread(mask, x):
    return jnp.where(mask, jnp.concatenate([x] * (mask.shape[0] // BLOCK), axis=0), jnp.zeros((), BF16))


def paired(mask, first, second):
    left = jnp.concatenate([spread(mask, first[0]), spread(mask, first[1])], axis=0)
    right = jnp.concatenate([spread(mask, second[0]), spread(mask, second[1])], axis=0)
    return jnp.concatenate([left, right], axis=1)


def stack_rows(parts):
    rows = []
    for part, is_low in parts:
        other = jnp.zeros_like(part) if is_low else part
        rows.append(jnp.concatenate([part, other], axis=1))
    return jnp.concatenate(rows, axis=0)


def rim_effect(key_taps, value_taps, edge, rim):
    k0, k1, v0, v1 = edge
    kb, ka, vb, va = rim
    base_k, base_v = key_taps[0] * k0, value_taps[0] * v0
    more_k, more_v = key_taps[1] * ka + key_taps[2] * kb, value_taps[1] * va + value_taps[2] * vb
    first = more_k * base_v + (base_k + more_k) * more_v
    base_k, base_v = key_taps[0] * k1 + key_taps[1] * k0, value_taps[0] * v1 + value_taps[1] * v0
    more_k, more_v = key_taps[2] * ka, value_taps[2] * va
    second = more_k * base_v + (base_k + more_k) * more_v
    return first, second


def main_kernel(
    count, streams, taps_in, rates, residues, skip_in,
    loc, query, forward_high, forward_low, incoming,
    xs, last, taps, skip, few_rates, few_amps, backward, u_high, u_low, first_rows,
    rim_out, rim_in, shifted, sums_out, sums_in, back_out, back_in,
    stream_sem, small_sem, rim_sems, sums_send, sums_recv, back_send, back_recv,
):
    rows, channels = loc.shape
    tiles = channels // LANES
    chunks = tiles // PER_CHUNK
    blocks = rows // BLOCK
    me = lax.axis_index("ctx")

    def stream_copy(s, c):
        return pltpu.make_async_copy(
            streams.at[:, pl.ds(pl.multiple_of(s * channels + c * WIDE, WIDE), WIDE)],
            xs.at[s, c], stream_sem.at[s, c])

    def chunk_at(k):
        return lax.rem(me // PER_CHUNK + 1 + k, chunks)

    small = [pltpu.make_async_copy(a, b, small_sem.at[i]) for i, (a, b) in enumerate((
        (rates, few_rates), (residues, few_amps), (taps_in, taps), (skip_in, skip),
        (streams.at[pl.ds(rows - BLOCK, BLOCK), :], last)))]
    for copy in small:
        copy.start()

    @pl.loop(0, chunks)
    def _(k):
        c = chunk_at(k)
        stream_copy(1, c).start()
        stream_copy(2, c).start()

    barrier = pltpu.get_barrier_semaphore()

    @pl.loop(1, count)
    def _(i):
        pl.semaphore_signal(barrier, inc=1, device_id={"ctx": lax.rem(me + i, count)}, device_id_type=MESH)

    @pl.loop(0, chunks)
    def _(k):
        stream_copy(0, chunk_at(k)).start()

    small[0].wait()
    small[1].wait()
    few = few_rates[...]
    few_amps[...] = few_amps[...] * (few * (1.0 - few / 2 * (1.0 - few / 3 * (1.0 - few / 4 * (
        1.0 - few / 5 * (1.0 - few / 6))))))

    def picked(ref, group, index):
        part = pl.ds(pl.multiple_of(group // LANES * LANES, LANES), LANES)
        return jnp.take_along_axis(ref[:, part], index + lax.rem(group, LANES), axis=1, mode="promise_in_bounds")

    @pl.loop(0, tiles // 2)
    def _(t):
        zero = jnp.zeros((BLOCK, LANES), jnp.int32)
        gap = LANES - 1.0 - lax.broadcasted_iota(jnp.int32, (BLOCK, LANES), 1).astype(F32)
        for g in range(PAIR // BLOCK):
            r = picked(few_rates, t * (PAIR // BLOCK) + g, zero)
            piece = jnp.exp(-r * gap)
            step = jnp.exp(-float(LANES) * r)
            pieces = [piece]
            for _ in range(rows // LANES - 1):
                pieces.append(pieces[-1] * step)
            for i, piece in enumerate(pieces[::-1]):
                high, low = halves(piece)
                backward[t, pl.ds(g * BLOCK, BLOCK), i * LANES:(i + 1) * LANES] = high
                backward[t, pl.ds(g * BLOCK, BLOCK), rows + i * LANES:rows + (i + 1) * LANES] = low

    for copy in small[2:]:
        copy.wait()

    rim_copy = pltpu.make_async_remote_copy(
        src_ref=rim_out, dst_ref=rim_in, send_sem=rim_sems.at[0], recv_sem=rim_sems.at[1],
        device_id={"ctx": lax.rem(me + 1, count)}, device_id_type=MESH)

    def shifted_rows(slot, s, c, j):
        lane = pl.ds(pl.multiple_of(j * LANES, LANES), LANES)
        shifted[slot, pl.ds(6, 2), :] = jnp.zeros((2, LANES), F32)
        for b in range(blocks):
            shifted[slot, pl.ds(8 + BLOCK * b, BLOCK), :] = xs[s, c, pl.ds(BLOCK * b, BLOCK), lane].astype(F32)

    def stream_taps(s, t):
        lane = pl.ds(pl.multiple_of(s * channels + t * LANES, LANES), LANES)
        return [taps[tap:tap + 1, lane] for tap in range(3)]

    def filtered(slot, by, b):
        total = by[0] * shifted[slot, pl.ds(8 + BLOCK * b, BLOCK), :]
        for tap in (1, 2):
            total = total + by[tap] * shifted[slot, pl.ds(8 + BLOCK * b - tap, BLOCK), :]
        return total

    def sums_copy(t):
        return pltpu.make_async_remote_copy(
            src_ref=sums_out.at[t], dst_ref=sums_in.at[me], send_sem=sums_send.at[t], recv_sem=sums_recv.at[me],
            device_id={"ctx": t}, device_id_type=MESH)

    def pair_at(k, i):
        return chunk_at(k), lax.rem(me // 2 + i, PER_CHUNK // 2)

    mask = group_mask(LANES)

    def sums_pair(k, i):
        c, p = pair_at(k, i)
        sides = []
        for side in range(2):
            j = 2 * p + side
            t = c * PER_CHUNK + j
            lane = pl.ds(pl.multiple_of(t * LANES, LANES), LANES)
            at_key, at_value = 2 * side, 2 * side + 1
            shifted_rows(at_key, 1, c, j)
            shifted_rows(at_value, 2, c, j)
            by_key, by_value = stream_taps(1, t), stream_taps(2, t)
            direct = skip[0:1, lane]
            highs, lows = [], []
            for b in range(blocks):
                at = pl.ds(b * BLOCK, BLOCK)
                inner = filtered(at_key, by_key, b) * filtered(at_value, by_value, b)
                loc[at, lane] = direct * inner
                high, low = halves(inner)
                u_high[at, lane] = high
                u_low[at, lane] = low
                highs.append(high)
                lows.append(low)
            sides.append((jnp.concatenate(highs, axis=0), jnp.concatenate(lows, axis=0)))
            end = 6 + rows
            sums_out[t, pl.ds(BLOCK, 2)] = shifted[at_key, pl.ds(8, 2), :]
            sums_out[t, pl.ds(BLOCK + 2, 2)] = shifted[at_value, pl.ds(8, 2), :]
            sums_out[t, pl.ds(BLOCK + 4, 2)] = shifted[at_key, pl.ds(end, 2), :]
            sums_out[t, pl.ds(BLOCK + 6, 2)] = shifted[at_value, pl.ds(end, 2), :]
        pair = c * (PER_CHUNK // 2) + p
        high, low = [jnp.concatenate([sides[0][i], sides[1][i]], axis=1) for i in range(2)]
        by = backward[pair]
        every = jnp.dot(jnp.concatenate([by, by[:, :rows]], axis=1), jnp.concatenate([high, high, low], axis=0),
                        preferred_element_type=F32)
        own = lax.broadcasted_iota(jnp.int32, (BLOCK, LANES), 1) // BLOCK
        for side in range(2):
            total = jnp.zeros((BLOCK, LANES), F32)
            for g in range(LANES // BLOCK):
                at = (side * (LANES // BLOCK) + g) * BLOCK
                total = jnp.where(own == g, every[at:at + BLOCK, side * LANES:(side + 1) * LANES], total)
            sums_out[c * PER_CHUNK + 2 * p + side, 0:BLOCK] = total

    def sums_chunk(k):
        c = chunk_at(k)
        stream_copy(1, c).wait()
        stream_copy(2, c).wait()

        @pl.loop(0, PER_CHUNK // 2)
        def _(i):
            sums_pair(k, i)

    def send_chunk(k):
        for i in range(PER_CHUNK // 2):
            c, p = pair_at(k, i)
            for side in range(2):
                t = c * PER_CHUNK + 2 * p + side

                @pl.when(t != me)
                def _():
                    sums_copy(t).start()

    greeted = chunks // 2

    @pl.loop(0, greeted)
    def _(k):
        sums_chunk(k)

    pl.semaphore_wait(barrier, count - 1)

    @pl.loop(0, greeted)
    def _(k):
        send_chunk(k)

    @pl.loop(greeted, chunks)
    def _(k):
        sums_chunk(k)
        send_chunk(k)

    sums_in[me] = sums_out[me]

    @pl.loop(0, 3 * chunks)
    def _(e):
        for p in range(PER_CHUNK):
            lane = pl.ds(pl.multiple_of(e * WIDE + p * LANES, LANES), LANES)
            rim_out[e, 2 * p:2 * p + 2, :] = last[:, lane].astype(F32)[BLOCK - 2:]

    rim_copy.start()

    @pl.loop(0, chunks)
    def _(k):
        stream_copy(0, chunk_at(k)).wait()

    def rest_tile(u, t):
        lane = pl.ds(pl.multiple_of(t * LANES, LANES), LANES)
        inside = lax.broadcasted_iota(jnp.int32, (BLOCK, LANES), 1) % BLOCK
        row = lax.broadcasted_iota(jnp.int32, (BLOCK, LANES), 0)
        pick = lax.broadcasted_iota(jnp.int32, (BLOCK, LANES), 1) // BLOCK
        group = t * (LANES // BLOCK)
        r, a = picked(few_rates, group, pick), picked(few_amps, group, pick)
        own = row == inside
        r_own = jnp.sum(jnp.where(own, r, 0.0), axis=0, keepdims=True)
        a_own = jnp.sum(jnp.where(own, a, 0.0), axis=0, keepdims=True)
        out = a_own * jnp.exp(-r_own * (row.astype(F32) + 1.0))
        step = jnp.exp(-float(BLOCK) * r_own)
        near = []
        for b in range(blocks):
            high, low = halves(out)
            forward_high[pl.ds(b * BLOCK, BLOCK), lane] = high
            forward_low[pl.ds(b * BLOCK, BLOCK), lane] = low
            if b < 2:
                near.append((high, low))
            out = out * step
        by = stack_rows([(near[0][0], False), (near[1][0], False), (near[0][1], True), (near[1][1], True)])
        inside = inside.astype(F32)
        high, low = halves(jnp.exp(r * (inside + 1.0)))
        span = jnp.dot(by, jnp.concatenate([spread(mask, high), spread(mask, low)], axis=0), preferred_element_type=F32)
        span = span[:SPAN] + span[SPAN:]
        near = halves(jnp.where(row.astype(F32) >= inside, span[:BLOCK], 0.0))
        far = halves(span[BLOCK:])
        back = halves(jnp.exp(-r * (BLOCK - 1.0 - inside)))
        weights = stack_rows([(far[0], False), (far[1], True), (near[0], False), (back[0], False),
                              (near[1], True), (back[1], True)])
        shifted_rows(u, 0, t // PER_CHUNK, lax.rem(t, PER_CHUNK))
        by_query = stream_taps(0, t)
        step = jnp.exp(-float(BLOCK) * r)
        state = jnp.zeros((BLOCK, LANES), F32)

        def block_u(b):
            at = pl.ds(b * BLOCK, BLOCK)
            return u_high[at, lane], u_low[at, lane]

        for quad in range(blocks // 4):
            even = jnp.dot(weights, paired(mask, block_u(4 * quad), block_u(4 * quad + 2)), preferred_element_type=F32)
            odd = jnp.dot(weights[2 * BLOCK:], paired(mask, block_u(4 * quad + 1), block_u(4 * quad + 3)),
                          preferred_element_type=F32)
            states, values = [], []
            for b in range(4):
                side = slice((b // 2) * LANES, (b // 2 + 1) * LANES)
                part = odd[:, side] if b % 2 else even[2 * BLOCK:, side]
                value = loc[pl.ds((4 * quad + b) * BLOCK, BLOCK), lane] + (part[:BLOCK] + part[2 * BLOCK:3 * BLOCK])
                if b % 2:
                    value = value + (even[:BLOCK, side] + even[BLOCK:2 * BLOCK, side])
                else:
                    states.append(halves(state))
                values.append(value)
                state = state * step + (part[BLOCK:2 * BLOCK] + part[3 * BLOCK:])
            both = jnp.dot(by, paired(mask, *states), preferred_element_type=F32)
            for b in range(4):
                value = both[:, (b // 2) * LANES:(b // 2 + 1) * LANES]
                half = (b % 2) * BLOCK
                total = values[b] + (value[half:half + BLOCK] + value[SPAN + half:SPAN + half + BLOCK])
                if quad == 0 and b == 0:
                    first_rows[t] = total[:8]
                at = pl.ds((4 * quad + b) * BLOCK, BLOCK)
                gate = filtered(u, by_query, 4 * quad + b)
                query[at, lane] = gate
                loc[at, lane] = gate * total

    answered = tiles // 2

    @pl.loop(0, answered, step=UNROLL)
    def _(t):
        for u in range(UNROLL):
            rest_tile(u, t + u)

    def sums_arrival(d):
        return pltpu.make_async_remote_copy(
            src_ref=sums_out.at[d], dst_ref=sums_in.at[d], send_sem=sums_send.at[d], recv_sem=sums_recv.at[d],
            device_id={"ctx": d}, device_id_type=MESH)

    def back_copy(d):
        return pltpu.make_async_remote_copy(
            src_ref=back_out.at[d], dst_ref=back_in.at[me], send_sem=back_send.at[d], recv_sem=back_recv.at[me],
            device_id={"ctx": d}, device_id_type=MESH)

    def back_arrival(d):
        return pltpu.make_async_remote_copy(
            src_ref=back_out.at[d], dst_ref=back_in.at[d], send_sem=back_send.at[d], recv_sem=back_recv.at[d],
            device_id={"ctx": d}, device_id_type=MESH)

    @pl.loop(1, count)
    def _(i):
        sums_arrival(lax.rem(me + i, count)).wait_recv()

    pick = lax.broadcasted_iota(jnp.int32, (BLOCK, LANES), 1) // BLOCK
    r = picked(few_rates, me * (LANES // BLOCK), pick)
    device_decay = jnp.exp(-float(rows) * r)
    ahead = jnp.exp(r)
    further = ahead * ahead
    key_taps, value_taps = stream_taps(1, me), stream_taps(2, me)
    state = jnp.zeros((BLOCK, LANES), F32)
    for d in range(count):
        if d:
            edge = sums_in[d, BLOCK:BLOCK + EDGES]
            rim = sums_in[d - 1, BLOCK:BLOCK + EDGES]
            first, second = rim_effect(key_taps, value_taps, [edge[i:i + 1] for i in range(4)],
                                       [rim[i:i + 1] for i in range(4, 8)])
            state = state + (ahead * first + further * second)
        back_out[d] = state
        state = state * device_decay + sums_in[d, 0:BLOCK]
    back_in[me] = back_out[me]

    @pl.loop(1, count)
    def _(i):
        back_copy(lax.rem(me + i, count)).start()

    @pl.loop(answered, tiles, step=UNROLL)
    def _(t):
        for u in range(UNROLL):
            rest_tile(u, t + u)

    rim_copy.wait()
    has_rim = jnp.where(me > 0, 1.0, 0.0)

    @pl.loop(0, chunks)
    def _(c):
        for j in range(PER_CHUNK):
            t = c * PER_CHUNK + j
            lane = pl.ds(pl.multiple_of(t * LANES, LANES), LANES)
            rim = [rim_in[s * chunks + c, 2 * j:2 * j + 2, :] * has_rim for s in range(3)]
            edge = sums_out[t, pl.ds(BLOCK, 4)]
            first, second = rim_effect(
                stream_taps(1, t), stream_taps(2, t), [edge[i:i + 1] for i in range(4)],
                [rim[1][0:1], rim[1][1:2], rim[2][0:1], rim[2][1:2]])
            r, a = picked(few_rates, t * (LANES // BLOCK), pick), picked(few_amps, t * (LANES // BLOCK), pick)
            before = jnp.sum(a * jnp.exp(r), axis=0, keepdims=True)
            direct = skip[0:1, lane]
            by_query = stream_taps(0, t)
            total = first_rows[t]
            gate = query[0:8, lane]
            gates = (gate[0:1] + by_query[1] * rim[0][1:2] + by_query[2] * rim[0][0:1],
                     gate[1:2] + by_query[2] * rim[0][1:2])
            totals = (total[0:1] + direct * first - before * second, total[1:2] + direct * second)
            for i in range(2):
                query[i:i + 1, lane] = gates[i]
                loc[i:i + 1, lane] = gates[i] * totals[i]

    @pl.loop(1, count)
    def _(i):
        d = lax.rem(me + i, count)
        back_arrival(d).wait_recv()
        sums_arrival(d).wait_send()
        back_copy(d).wait_send()

    for t in range(tiles):
        incoming[:, t * LANES:(t + 1) * LANES] = back_in[t]


def last_kernel(loc, query, forward_high, forward_low, incoming, out, held, sems):
    channels = loc.shape[1]
    mask = group_mask(PAIR)
    copies = []
    for start in range(0, channels, WIDE):
        for first in range(start, start + WIDE, PAIR):
            lane = slice(first, first + PAIR)
            high, low = halves(incoming[:, lane])
            high, low = spread(mask, high), spread(mask, low)
            by_high, by_low = forward_high[:, lane], forward_low[:, lane]
            value = jnp.dot(jnp.concatenate([by_high, by_low, by_high], axis=1),
                            jnp.concatenate([high, high, low], axis=0), preferred_element_type=F32)
            held[:, lane] = loc[:, lane] + query[:, lane] * value
        lane = slice(start, start + WIDE)
        copies.append(pltpu.make_async_copy(held.at[:, lane], out.at[:, lane], sems.at[start // WIDE]))
        copies[-1].start()
    for copy in copies:
        copy.wait()


def body(count, streams, short_filter, rates, residues, skip):
    rows = streams.shape[0]
    channels = skip.shape[0]
    groups = rates.shape[0]
    tiles = channels // LANES
    chunks = tiles // PER_CHUNK
    vmem = pl.BlockSpec(memory_space=pltpu.VMEM)
    hbm = pl.BlockSpec(memory_space=pltpu.HBM)
    shapes = (
        ((rows, channels), F32),
        ((rows, channels), F32),
        ((rows, channels), BF16),
        ((rows, channels), BF16),
        ((BLOCK, channels), F32),
    )
    operands = (streams, short_filter, rates.T, residues.T, skip[None, :])
    operands = [pltpu.with_memory_space_constraint(x, pltpu.HBM) for x in operands]
    parts = pl.pallas_call(
        functools.partial(main_kernel, count),
        out_shape=tuple(pltpu.VMEM(shape, dtype) for shape, dtype in shapes),
        in_specs=[hbm] * 5,
        out_specs=(vmem,) * len(shapes),
        scratch_shapes=[
            pltpu.VMEM((3, chunks, rows, WIDE), BF16),
            pltpu.VMEM((BLOCK, 3 * channels), BF16),
            pltpu.VMEM(short_filter.shape, F32),
            pltpu.VMEM((1, channels), F32),
            pltpu.VMEM((BLOCK, groups), F32),
            pltpu.VMEM((BLOCK, groups), F32),
            pltpu.VMEM((tiles // 2, PAIR, 2 * rows), BF16),
            pltpu.VMEM((rows, channels), BF16),
            pltpu.VMEM((rows, channels), BF16),
            pltpu.VMEM((tiles, 8, LANES), F32),
            pltpu.VMEM((3 * chunks, 8, LANES), F32),
            pltpu.VMEM((3 * chunks, 8, LANES), F32),
            pltpu.VMEM((4, rows + 8, LANES), F32),
            pltpu.VMEM((count, BLOCK + EDGES, LANES), F32),
            pltpu.VMEM((count, BLOCK + EDGES, LANES), F32),
            pltpu.VMEM((count, BLOCK, LANES), F32),
            pltpu.VMEM((count, BLOCK, LANES), F32),
            pltpu.SemaphoreType.DMA((3, chunks)),
            pltpu.SemaphoreType.DMA((5,)),
            pltpu.SemaphoreType.DMA((2,)),
            pltpu.SemaphoreType.DMA((count,)),
            pltpu.SemaphoreType.DMA((count,)),
            pltpu.SemaphoreType.DMA((count,)),
            pltpu.SemaphoreType.DMA((count,)),
        ],
        compiler_params=pltpu.CompilerParams(
            collective_id=0, has_side_effects=True, vmem_limit_bytes=24 << 20),
        name="local_part",
    )(*operands)
    parts = [pltpu.with_memory_space_constraint(part, pltpu.VMEM) for part in parts]
    return pl.pallas_call(
        last_kernel,
        out_shape=jax.ShapeDtypeStruct((rows, channels), F32),
        in_specs=[vmem] * len(parts),
        out_specs=hbm,
        scratch_shapes=[pltpu.VMEM((rows, channels), F32), pltpu.SemaphoreType.DMA((chunks,))],
        compiler_params=pltpu.CompilerParams(vmem_limit_bytes=16 << 20),
        name="carried_part",
    )(*parts)


def solution(mesh):
    count = mesh.shape["ctx"]
    in_specs = (P(("dp", "ctx"), None), P(), P(), P(), P())
    out_specs = P(("dp", "ctx"), None)
    return jax.shard_map(functools.partial(body, count), mesh=mesh, in_specs=in_specs, out_specs=out_specs,
                         check_vma=False)
```

```python
import functools

import jax
import jax.numpy as jnp
from jax import lax
from jax.experimental import pallas as pl
from jax.experimental.pallas import tpu as pltpu
from jax.sharding import PartitionSpec as P

F32 = jnp.float32
BF16 = jnp.bfloat16
LANES = 128
BLOCK = 16
SPAN = 2 * BLOCK
PER_CHUNK = 4
WIDE = PER_CHUNK * LANES
EDGES = 8
PAIR = 2 * LANES
UNROLL = 4
MESH = pl.DeviceIdType.MESH


def halves(x):
    high = x.astype(BF16)
    return high, (x - high.astype(F32)).astype(BF16)


def group_mask(lanes):
    row = lax.broadcasted_iota(jnp.int32, (lanes, lanes), 0) // BLOCK
    lane = lax.broadcasted_iota(jnp.int32, (lanes, lanes), 1) // BLOCK
    return row == lane


def spread(mask, x):
    return jnp.where(mask, jnp.concatenate([x] * (mask.shape[0] // BLOCK), axis=0), jnp.zeros((), BF16))


def paired(mask, first, second):
    left = jnp.concatenate([spread(mask, first[0]), spread(mask, first[1])], axis=0)
    right = jnp.concatenate([spread(mask, second[0]), spread(mask, second[1])], axis=0)
    return jnp.concatenate([left, right], axis=1)


def stack_rows(parts):
    rows = []
    for part, is_low in parts:
        other = jnp.zeros_like(part) if is_low else part
        rows.append(jnp.concatenate([part, other], axis=1))
    return jnp.concatenate(rows, axis=0)


def rim_effect(key_taps, value_taps, edge, rim):
    k0, k1, v0, v1 = edge
    kb, ka, vb, va = rim
    base_k, base_v = key_taps[0] * k0, value_taps[0] * v0
    more_k, more_v = key_taps[1] * ka + key_taps[2] * kb, value_taps[1] * va + value_taps[2] * vb
    first = more_k * base_v + (base_k + more_k) * more_v
    base_k, base_v = key_taps[0] * k1 + key_taps[1] * k0, value_taps[0] * v1 + value_taps[1] * v0
    more_k, more_v = key_taps[2] * ka, value_taps[2] * va
    second = more_k * base_v + (base_k + more_k) * more_v
    return first, second


def main_kernel(
    count, streams, taps_in, rates, residues, skip_in,
    loc, query, forward_high, forward_low, incoming,
    xs, last, taps, skip, few_rates, few_amps, backward, u_high, u_low, first_rows,
    weights, states, rim_out, rim_in, shifted, sums_out, sums_in, back_out, back_in,
    stream_sem, small_sem, rim_sems, sums_send, sums_recv, back_send, back_recv,
):
    rows, channels = loc.shape
    tiles = channels // LANES
    chunks = tiles // PER_CHUNK
    blocks = rows // BLOCK
    me = lax.axis_index("ctx")

    def stream_copy(s, c):
        return pltpu.make_async_copy(
            streams.at[:, pl.ds(pl.multiple_of(s * channels + c * WIDE, WIDE), WIDE)],
            xs.at[s, c], stream_sem.at[s, c])

    def chunk_at(k):
        return lax.rem(me // PER_CHUNK + 1 + k, chunks)

    small = [pltpu.make_async_copy(a, b, small_sem.at[i]) for i, (a, b) in enumerate((
        (rates, few_rates), (residues, few_amps), (taps_in, taps), (skip_in, skip),
        (streams.at[pl.ds(rows - BLOCK, BLOCK), :], last)))]
    for copy in small:
        copy.start()

    @pl.loop(0, chunks)
    def _(k):
        c = chunk_at(k)
        stream_copy(1, c).start()
        stream_copy(2, c).start()

    barrier = pltpu.get_barrier_semaphore()

    @pl.loop(1, count)
    def _(i):
        pl.semaphore_signal(barrier, inc=1, device_id={"ctx": lax.rem(me + i, count)}, device_id_type=MESH)

    @pl.loop(0, chunks)
    def _(k):
        stream_copy(0, chunk_at(k)).start()

    small[0].wait()
    small[1].wait()
    few = few_rates[...]
    few_amps[...] = few_amps[...] * (few * (1.0 - few / 2 * (1.0 - few / 3 * (1.0 - few / 4 * (
        1.0 - few / 5 * (1.0 - few / 6))))))

    def picked(ref, group, index):
        part = pl.ds(pl.multiple_of(group // LANES * LANES, LANES), LANES)
        return jnp.take_along_axis(ref[:, part], index + lax.rem(group, LANES), axis=1, mode="promise_in_bounds")

    @pl.loop(0, tiles // 2)
    def _(t):
        zero = jnp.zeros((BLOCK, LANES), jnp.int32)
        gap = LANES - 1.0 - lax.broadcasted_iota(jnp.int32, (BLOCK, LANES), 1).astype(F32)
        for g in range(PAIR // BLOCK):
            r = picked(few_rates, t * (PAIR // BLOCK) + g, zero)
            piece = jnp.exp(-r * gap)
            step = jnp.exp(-float(LANES) * r)
            pieces = [piece]
            for _ in range(rows // LANES - 1):
                pieces.append(pieces[-1] * step)
            for i, piece in enumerate(pieces[::-1]):
                high, low = halves(piece)
                backward[t, pl.ds(g * BLOCK, BLOCK), i * LANES:(i + 1) * LANES] = high
                backward[t, pl.ds(g * BLOCK, BLOCK), rows + i * LANES:rows + (i + 1) * LANES] = low

    for copy in small[2:]:
        copy.wait()

    rim_copy = pltpu.make_async_remote_copy(
        src_ref=rim_out, dst_ref=rim_in, send_sem=rim_sems.at[0], recv_sem=rim_sems.at[1],
        device_id={"ctx": lax.rem(me + 1, count)}, device_id_type=MESH)

    def shifted_rows(slot, s, c, j):
        lane = pl.ds(pl.multiple_of(j * LANES, LANES), LANES)
        shifted[slot, pl.ds(6, 2), :] = jnp.zeros((2, LANES), F32)
        for b in range(blocks):
            shifted[slot, pl.ds(8 + BLOCK * b, BLOCK), :] = xs[s, c, pl.ds(BLOCK * b, BLOCK), lane].astype(F32)

    def stream_taps(s, t):
        lane = pl.ds(pl.multiple_of(s * channels + t * LANES, LANES), LANES)
        return [taps[tap:tap + 1, lane] for tap in range(3)]

    def filtered(slot, by, b):
        total = by[0] * shifted[slot, pl.ds(8 + BLOCK * b, BLOCK), :]
        for tap in (1, 2):
            total = total + by[tap] * shifted[slot, pl.ds(8 + BLOCK * b - tap, BLOCK), :]
        return total

    def sums_copy(t):
        return pltpu.make_async_remote_copy(
            src_ref=sums_out.at[t], dst_ref=sums_in.at[me], send_sem=sums_send.at[t], recv_sem=sums_recv.at[me],
            device_id={"ctx": t}, device_id_type=MESH)

    halfs = PER_CHUNK // 2

    def pair_at(q):
        return chunk_at(q // halfs), lax.rem(me // 2 + lax.rem(q, halfs), halfs)

    mask = group_mask(LANES)

    def values_pair(q):
        c, p = pair_at(q)
        for side in range(2):
            j = 2 * p + side
            t = c * PER_CHUNK + j
            lane = pl.ds(pl.multiple_of(t * LANES, LANES), LANES)
            at_key, at_value = 2 * side, 2 * side + 1
            shifted_rows(at_key, 1, c, j)
            shifted_rows(at_value, 2, c, j)
            by_key, by_value = stream_taps(1, t), stream_taps(2, t)
            direct = skip[0:1, lane]
            for b in range(blocks):
                at = pl.ds(b * BLOCK, BLOCK)
                inner = filtered(at_key, by_key, b) * filtered(at_value, by_value, b)
                loc[at, lane] = direct * inner
                u_high[at, lane], u_low[at, lane] = halves(inner)
            end = 6 + rows
            sums_out[t, pl.ds(BLOCK, 2)] = shifted[at_key, pl.ds(8, 2), :]
            sums_out[t, pl.ds(BLOCK + 2, 2)] = shifted[at_value, pl.ds(8, 2), :]
            sums_out[t, pl.ds(BLOCK + 4, 2)] = shifted[at_key, pl.ds(end, 2), :]
            sums_out[t, pl.ds(BLOCK + 6, 2)] = shifted[at_value, pl.ds(end, 2), :]

    def sums_pair(q):
        c, p = pair_at(q)
        pair = c * halfs + p
        lane = pl.ds(pl.multiple_of(pair * PAIR, PAIR), PAIR)
        high, low = u_high[:, lane], u_low[:, lane]
        by = backward[pair]
        every = jnp.dot(jnp.concatenate([by, by[:, :rows]], axis=1), jnp.concatenate([high, high, low], axis=0),
                        preferred_element_type=F32)
        own = lax.broadcasted_iota(jnp.int32, (BLOCK, LANES), 1) // BLOCK
        for side in range(2):
            total = jnp.zeros((BLOCK, LANES), F32)
            for g in range(LANES // BLOCK):
                at = (side * (LANES // BLOCK) + g) * BLOCK
                total = jnp.where(own == g, every[at:at + BLOCK, side * LANES:(side + 1) * LANES], total)
            sums_out[2 * pair + side, 0:BLOCK] = total

    def send_pair(q):
        c, p = pair_at(q)
        for side in range(2):
            t = c * PER_CHUNK + 2 * p + side

            @pl.when(t != me)
            def _():
                sums_copy(t).start()

    def chunk_wait(q):
        @pl.when(lax.rem(q, halfs) == 0)
        def _():
            c = chunk_at(q // halfs)
            stream_copy(1, c).wait()
            stream_copy(2, c).wait()

    pairs = tiles // 2
    greeted = pairs // 2
    chunk_wait(0)
    values_pair(0)

    @pl.loop(1, greeted)
    def _(q):
        chunk_wait(q)
        sums_pair(q - 1)
        values_pair(q)

    pl.semaphore_wait(barrier, count - 1)

    @pl.loop(0, greeted - 1)
    def _(q):
        send_pair(q)

    @pl.loop(greeted, pairs)
    def _(q):
        chunk_wait(q)
        sums_pair(q - 1)
        values_pair(q)
        send_pair(q - 1)

    sums_pair(pairs - 1)
    send_pair(pairs - 1)
    sums_in[me] = sums_out[me]

    @pl.loop(0, 3 * chunks)
    def _(e):
        for p in range(PER_CHUNK):
            lane = pl.ds(pl.multiple_of(e * WIDE + p * LANES, LANES), LANES)
            rim_out[e, 2 * p:2 * p + 2, :] = last[:, lane].astype(F32)[BLOCK - 2:]

    rim_copy.start()

    @pl.loop(0, chunks)
    def _(k):
        stream_copy(0, chunk_at(k)).wait()

    pick = lax.broadcasted_iota(jnp.int32, (BLOCK, LANES), 1) // BLOCK
    groups = LANES // BLOCK

    def filters_stage(u, t):
        lane = pl.ds(pl.multiple_of(t * LANES, LANES), LANES)
        inside = lax.broadcasted_iota(jnp.int32, (BLOCK, LANES), 1) % BLOCK
        row = lax.broadcasted_iota(jnp.int32, (BLOCK, LANES), 0)
        r, a = picked(few_rates, t * groups, pick), picked(few_amps, t * groups, pick)
        own = row == inside
        r_own = jnp.sum(jnp.where(own, r, 0.0), axis=0, keepdims=True)
        a_own = jnp.sum(jnp.where(own, a, 0.0), axis=0, keepdims=True)
        out = a_own * jnp.exp(-r_own * (row.astype(F32) + 1.0))
        step = jnp.exp(-float(BLOCK) * r_own)
        near = []
        for b in range(blocks):
            high, low = halves(out)
            forward_high[pl.ds(b * BLOCK, BLOCK), lane] = high
            forward_low[pl.ds(b * BLOCK, BLOCK), lane] = low
            if b < 2:
                near.append((high, low))
            out = out * step
        by = stack_rows([(near[0][0], False), (near[1][0], False), (near[0][1], True), (near[1][1], True)])
        inside = inside.astype(F32)
        high, low = halves(jnp.exp(r * (inside + 1.0)))
        span = jnp.dot(by, jnp.concatenate([spread(mask, high), spread(mask, low)], axis=0), preferred_element_type=F32)
        span = span[:SPAN] + span[SPAN:]
        near = halves(jnp.where(row.astype(F32) >= inside, span[:BLOCK], 0.0))
        far = halves(span[BLOCK:])
        back = halves(jnp.exp(-r * (BLOCK - 1.0 - inside)))
        weights[u] = stack_rows([(far[0], False), (far[1], True), (near[0], False), (back[0], False),
                                 (near[1], True), (back[1], True)])

    def near_stage(u, t):
        lane = pl.ds(pl.multiple_of(t * LANES, LANES), LANES)
        step = jnp.exp(-float(BLOCK) * picked(few_rates, t * groups, pick))
        by = weights[u]

        def block_u(b):
            at = pl.ds(b * BLOCK, BLOCK)
            return u_high[at, lane], u_low[at, lane]

        products = []
        for quad in range(blocks // 4):
            products.append((
                jnp.dot(by, paired(mask, block_u(4 * quad), block_u(4 * quad + 2)), preferred_element_type=F32),
                jnp.dot(by[2 * BLOCK:], paired(mask, block_u(4 * quad + 1), block_u(4 * quad + 3)),
                        preferred_element_type=F32)))
        state = jnp.zeros((BLOCK, LANES), F32)
        for b in range(blocks):
            even, odd = products[b // 4]
            side = slice((b % 4 // 2) * LANES, (b % 4 // 2 + 1) * LANES)
            part = odd[:, side] if b % 2 else even[2 * BLOCK:, side]
            value = part[:BLOCK] + part[2 * BLOCK:3 * BLOCK]
            if b % 2:
                value = value + (even[:BLOCK, side] + even[BLOCK:2 * BLOCK, side])
            else:
                states[u, b // 2, 0], states[u, b // 2, 1] = halves(state)
            loc[pl.ds(b * BLOCK, BLOCK), lane] += value
            state = state * step + (part[BLOCK:2 * BLOCK] + part[3 * BLOCK:])

    def gate_stage(u, t):
        lane = pl.ds(pl.multiple_of(t * LANES, LANES), LANES)
        low = forward_low[0:SPAN, lane]
        by = stack_rows([(forward_high[0:SPAN, lane], False), (low, True)])
        products = [jnp.dot(by, paired(mask, (states[u, m, 0], states[u, m, 1]), (states[u, m + 1, 0], states[u, m + 1, 1])),
                            preferred_element_type=F32) for m in range(0, rows // SPAN, 2)]
        shifted_rows(u, 0, t // PER_CHUNK, lax.rem(t, PER_CHUNK))
        by_query = stream_taps(0, t)
        for b in range(blocks):
            at = pl.ds(b * BLOCK, BLOCK)
            value = products[b // 4][:, (b % 4 // 2) * LANES:(b % 4 // 2 + 1) * LANES]
            half = (b % 2) * BLOCK
            total = loc[at, lane] + (value[half:half + BLOCK] + value[SPAN + half:SPAN + half + BLOCK])
            if b == 0:
                first_rows[t] = total[:8]
            gate = filtered(u, by_query, b)
            query[at, lane] = gate
            loc[at, lane] = gate * total

    def stages(i, which):
        for stage, back in ((gate_stage, 2), (near_stage, 1), (filters_stage, 0)):
            if back in which:
                for u in range(UNROLL):
                    stage(u, (i - back) * UNROLL + u)

    steps = tiles // UNROLL
    answered = steps // 2
    stages(0, (0,))
    stages(1, (0, 1))

    @pl.loop(2, answered)
    def _(i):
        stages(i, (0, 1, 2))

    def sums_arrival(d):
        return pltpu.make_async_remote_copy(
            src_ref=sums_out.at[d], dst_ref=sums_in.at[d], send_sem=sums_send.at[d], recv_sem=sums_recv.at[d],
            device_id={"ctx": d}, device_id_type=MESH)

    def back_copy(d):
        return pltpu.make_async_remote_copy(
            src_ref=back_out.at[d], dst_ref=back_in.at[me], send_sem=back_send.at[d], recv_sem=back_recv.at[me],
            device_id={"ctx": d}, device_id_type=MESH)

    def back_arrival(d):
        return pltpu.make_async_remote_copy(
            src_ref=back_out.at[d], dst_ref=back_in.at[d], send_sem=back_send.at[d], recv_sem=back_recv.at[d],
            device_id={"ctx": d}, device_id_type=MESH)

    @pl.loop(1, count)
    def _(i):
        sums_arrival(lax.rem(me + i, count)).wait_recv()

    r = picked(few_rates, me * groups, pick)
    device_decay = jnp.exp(-float(rows) * r)
    ahead = jnp.exp(r)
    further = ahead * ahead
    key_taps, value_taps = stream_taps(1, me), stream_taps(2, me)
    state = jnp.zeros((BLOCK, LANES), F32)
    for d in range(count):
        if d:
            edge = sums_in[d, BLOCK:BLOCK + EDGES]
            rim = sums_in[d - 1, BLOCK:BLOCK + EDGES]
            first, second = rim_effect(key_taps, value_taps, [edge[i:i + 1] for i in range(4)],
                                       [rim[i:i + 1] for i in range(4, 8)])
            state = state + (ahead * first + further * second)
        back_out[d] = state
        state = state * device_decay + sums_in[d, 0:BLOCK]
    back_in[me] = back_out[me]

    @pl.loop(1, count)
    def _(i):
        back_copy(lax.rem(me + i, count)).start()

    @pl.loop(answered, steps)
    def _(i):
        stages(i, (0, 1, 2))

    stages(steps, (1, 2))
    stages(steps + 1, (2,))

    rim_copy.wait()
    has_rim = jnp.where(me > 0, 1.0, 0.0)

    @pl.loop(0, chunks)
    def _(c):
        for j in range(PER_CHUNK):
            t = c * PER_CHUNK + j
            lane = pl.ds(pl.multiple_of(t * LANES, LANES), LANES)
            rim = [rim_in[s * chunks + c, 2 * j:2 * j + 2, :] * has_rim for s in range(3)]
            edge = sums_out[t, pl.ds(BLOCK, 4)]
            first, second = rim_effect(
                stream_taps(1, t), stream_taps(2, t), [edge[i:i + 1] for i in range(4)],
                [rim[1][0:1], rim[1][1:2], rim[2][0:1], rim[2][1:2]])
            r, a = picked(few_rates, t * groups, pick), picked(few_amps, t * groups, pick)
            before = jnp.sum(a * jnp.exp(r), axis=0, keepdims=True)
            direct = skip[0:1, lane]
            by_query = stream_taps(0, t)
            total = first_rows[t]
            gate = query[0:8, lane]
            gates = (gate[0:1] + by_query[1] * rim[0][1:2] + by_query[2] * rim[0][0:1],
                     gate[1:2] + by_query[2] * rim[0][1:2])
            totals = (total[0:1] + direct * first - before * second, total[1:2] + direct * second)
            for i in range(2):
                query[i:i + 1, lane] = gates[i]
                loc[i:i + 1, lane] = gates[i] * totals[i]

    @pl.loop(1, count)
    def _(i):
        d = lax.rem(me + i, count)
        back_arrival(d).wait_recv()
        sums_arrival(d).wait_send()
        back_copy(d).wait_send()

    for t in range(tiles):
        incoming[:, t * LANES:(t + 1) * LANES] = back_in[t]


def last_kernel(loc, query, forward_high, forward_low, incoming, out, held, sems):
    channels = loc.shape[1]
    mask = group_mask(PAIR)
    copies = []
    for start in range(0, channels, WIDE):
        for first in range(start, start + WIDE, PAIR):
            lane = slice(first, first + PAIR)
            high, low = halves(incoming[:, lane])
            high, low = spread(mask, high), spread(mask, low)
            by_high, by_low = forward_high[:, lane], forward_low[:, lane]
            value = jnp.dot(jnp.concatenate([by_high, by_low, by_high], axis=1),
                            jnp.concatenate([high, high, low], axis=0), preferred_element_type=F32)
            held[:, lane] = loc[:, lane] + query[:, lane] * value
        lane = slice(start, start + WIDE)
        copies.append(pltpu.make_async_copy(held.at[:, lane], out.at[:, lane], sems.at[start // WIDE]))
        copies[-1].start()
    for copy in copies:
        copy.wait()


def body(count, streams, short_filter, rates, residues, skip):
    rows = streams.shape[0]
    channels = skip.shape[0]
    groups = rates.shape[0]
    tiles = channels // LANES
    chunks = tiles // PER_CHUNK
    vmem = pl.BlockSpec(memory_space=pltpu.VMEM)
    hbm = pl.BlockSpec(memory_space=pltpu.HBM)
    shapes = (
        ((rows, channels), F32),
        ((rows, channels), F32),
        ((rows, channels), BF16),
        ((rows, channels), BF16),
        ((BLOCK, channels), F32),
    )
    operands = (streams, short_filter, rates.T, residues.T, skip[None, :])
    operands = [pltpu.with_memory_space_constraint(x, pltpu.HBM) for x in operands]
    parts = pl.pallas_call(
        functools.partial(main_kernel, count),
        out_shape=tuple(pltpu.VMEM(shape, dtype) for shape, dtype in shapes),
        in_specs=[hbm] * 5,
        out_specs=(vmem,) * len(shapes),
        scratch_shapes=[
            pltpu.VMEM((3, chunks, rows, WIDE), BF16),
            pltpu.VMEM((BLOCK, 3 * channels), BF16),
            pltpu.VMEM(short_filter.shape, F32),
            pltpu.VMEM((1, channels), F32),
            pltpu.VMEM((BLOCK, groups), F32),
            pltpu.VMEM((BLOCK, groups), F32),
            pltpu.VMEM((tiles // 2, PAIR, 2 * rows), BF16),
            pltpu.VMEM((rows, channels), BF16),
            pltpu.VMEM((rows, channels), BF16),
            pltpu.VMEM((tiles, 8, LANES), F32),
            pltpu.VMEM((UNROLL, 6 * BLOCK, PAIR), BF16),
            pltpu.VMEM((UNROLL, rows // SPAN, 2, BLOCK, LANES), BF16),
            pltpu.VMEM((3 * chunks, 8, LANES), F32),
            pltpu.VMEM((3 * chunks, 8, LANES), F32),
            pltpu.VMEM((max(4, UNROLL), rows + 8, LANES), F32),
            pltpu.VMEM((count, BLOCK + EDGES, LANES), F32),
            pltpu.VMEM((count, BLOCK + EDGES, LANES), F32),
            pltpu.VMEM((count, BLOCK, LANES), F32),
            pltpu.VMEM((count, BLOCK, LANES), F32),
            pltpu.SemaphoreType.DMA((3, chunks)),
            pltpu.SemaphoreType.DMA((5,)),
            pltpu.SemaphoreType.DMA((2,)),
            pltpu.SemaphoreType.DMA((count,)),
            pltpu.SemaphoreType.DMA((count,)),
            pltpu.SemaphoreType.DMA((count,)),
            pltpu.SemaphoreType.DMA((count,)),
        ],
        compiler_params=pltpu.CompilerParams(
            collective_id=0, has_side_effects=True, vmem_limit_bytes=24 << 20),
        name="local_part",
    )(*operands)
    parts = [pltpu.with_memory_space_constraint(part, pltpu.VMEM) for part in parts]
    return pl.pallas_call(
        last_kernel,
        out_shape=jax.ShapeDtypeStruct((rows, channels), F32),
        in_specs=[vmem] * len(parts),
        out_specs=hbm,
        scratch_shapes=[pltpu.VMEM((rows, channels), F32), pltpu.SemaphoreType.DMA((chunks,))],
        compiler_params=pltpu.CompilerParams(vmem_limit_bytes=16 << 20),
        name="carried_part",
    )(*parts)


def solution(mesh):
    count = mesh.shape["ctx"]
    in_specs = (P(("dp", "ctx"), None), P(), P(), P(), P())
    out_specs = P(("dp", "ctx"), None)
    return jax.shard_map(functools.partial(body, count), mesh=mesh, in_specs=in_specs, out_specs=out_specs,
                         check_vma=False)
```

```python
import functools

import jax
import jax.numpy as jnp
from jax import lax
from jax.experimental import pallas as pl
from jax.experimental.pallas import tpu as pltpu
from jax.sharding import PartitionSpec as P

F32 = jnp.float32
BF16 = jnp.bfloat16
LANES = 128
BLOCK = 16
SPAN = 2 * BLOCK
PER_CHUNK = 4
WIDE = PER_CHUNK * LANES
EDGES = 8
PAIR = 2 * LANES
UNROLL = 4
MESH = pl.DeviceIdType.MESH


def halves(x):
    high = x.astype(BF16)
    return high, (x - high.astype(F32)).astype(BF16)


def group_mask(lanes):
    row = lax.broadcasted_iota(jnp.int32, (lanes, lanes), 0) // BLOCK
    lane = lax.broadcasted_iota(jnp.int32, (lanes, lanes), 1) // BLOCK
    return row == lane


def spread(mask, x):
    return jnp.where(mask, jnp.concatenate([x] * (mask.shape[0] // BLOCK), axis=0), jnp.zeros((), BF16))


def paired(mask, first, second):
    left = jnp.concatenate([spread(mask, first[0]), spread(mask, first[1])], axis=0)
    right = jnp.concatenate([spread(mask, second[0]), spread(mask, second[1])], axis=0)
    return jnp.concatenate([left, right], axis=1)


def stack_rows(parts):
    rows = []
    for part, is_low in parts:
        other = jnp.zeros_like(part) if is_low else part
        rows.append(jnp.concatenate([part, other], axis=1))
    return jnp.concatenate(rows, axis=0)


def rim_effect(key_taps, value_taps, edge, rim):
    k0, k1, v0, v1 = edge
    kb, ka, vb, va = rim
    base_k, base_v = key_taps[0] * k0, value_taps[0] * v0
    more_k, more_v = key_taps[1] * ka + key_taps[2] * kb, value_taps[1] * va + value_taps[2] * vb
    first = more_k * base_v + (base_k + more_k) * more_v
    base_k, base_v = key_taps[0] * k1 + key_taps[1] * k0, value_taps[0] * v1 + value_taps[1] * v0
    more_k, more_v = key_taps[2] * ka, value_taps[2] * va
    second = more_k * base_v + (base_k + more_k) * more_v
    return first, second


def main_kernel(
    count, streams, taps_in, rates, residues, skip_in,
    loc, query, forward_high, forward_low, incoming,
    xs, last, taps, skip, few_rates, few_amps, backward, u_high, u_low, first_rows,
    weights, states, rim_out, rim_in, shifted, sums_out, sums_in, back_out, back_in,
    stream_sem, small_sem, rim_sems, sums_send, sums_recv, back_send, back_recv,
):
    rows, channels = loc.shape
    tiles = channels // LANES
    chunks = tiles // PER_CHUNK
    blocks = rows // BLOCK
    me = lax.axis_index("ctx")

    def stream_copy(s, c):
        return pltpu.make_async_copy(
            streams.at[:, pl.ds(pl.multiple_of(s * channels + c * WIDE, WIDE), WIDE)],
            xs.at[s, c], stream_sem.at[s, c])

    def chunk_at(k):
        return lax.rem(me // PER_CHUNK + 1 + k, chunks)

    small = [pltpu.make_async_copy(a, b, small_sem.at[i]) for i, (a, b) in enumerate((
        (rates, few_rates), (residues, few_amps), (taps_in, taps), (skip_in, skip),
        (streams.at[pl.ds(rows - BLOCK, BLOCK), :], last)))]
    for copy in small:
        copy.start()

    @pl.loop(0, chunks)
    def _(k):
        c = chunk_at(k)
        stream_copy(1, c).start()
        stream_copy(2, c).start()

    barrier = pltpu.get_barrier_semaphore()

    @pl.loop(1, count)
    def _(i):
        pl.semaphore_signal(barrier, inc=1, device_id={"ctx": lax.rem(me + i, count)}, device_id_type=MESH)


    small[0].wait()
    small[1].wait()
    few = few_rates[...]
    few_amps[...] = few_amps[...] * (few * (1.0 - few / 2 * (1.0 - few / 3 * (1.0 - few / 4 * (
        1.0 - few / 5 * (1.0 - few / 6))))))

    def picked(ref, group, index):
        part = pl.ds(pl.multiple_of(group // LANES * LANES, LANES), LANES)
        return jnp.take_along_axis(ref[:, part], index + lax.rem(group, LANES), axis=1, mode="promise_in_bounds")

    def backward_pair(q):
        c, p = pair_at(q)
        t = c * halfs + p
        zero = jnp.zeros((BLOCK, LANES), jnp.int32)
        gap = LANES - 1.0 - lax.broadcasted_iota(jnp.int32, (BLOCK, LANES), 1).astype(F32)
        for g in range(PAIR // BLOCK):
            r = picked(few_rates, t * (PAIR // BLOCK) + g, zero)
            piece = jnp.exp(-r * gap)
            step = jnp.exp(-float(LANES) * r)
            pieces = [piece]
            for _ in range(rows // LANES - 1):
                pieces.append(pieces[-1] * step)
            for i, piece in enumerate(pieces[::-1]):
                high, low = halves(piece)
                backward[t, pl.ds(g * BLOCK, BLOCK), i * LANES:(i + 1) * LANES] = high
                backward[t, pl.ds(g * BLOCK, BLOCK), rows + i * LANES:rows + (i + 1) * LANES] = low

    for copy in small[2:]:
        copy.wait()

    rim_copy = pltpu.make_async_remote_copy(
        src_ref=rim_out, dst_ref=rim_in, send_sem=rim_sems.at[0], recv_sem=rim_sems.at[1],
        device_id={"ctx": lax.rem(me + 1, count)}, device_id_type=MESH)

    def shifted_rows(slot, s, c, j):
        lane = pl.ds(pl.multiple_of(j * LANES, LANES), LANES)
        shifted[slot, pl.ds(6, 2), :] = jnp.zeros((2, LANES), F32)
        for b in range(blocks):
            shifted[slot, pl.ds(8 + BLOCK * b, BLOCK), :] = xs[s, c, pl.ds(BLOCK * b, BLOCK), lane].astype(F32)

    def stream_taps(s, t):
        lane = pl.ds(pl.multiple_of(s * channels + t * LANES, LANES), LANES)
        return [taps[tap:tap + 1, lane] for tap in range(3)]

    def filtered(slot, by, b):
        total = by[0] * shifted[slot, pl.ds(8 + BLOCK * b, BLOCK), :]
        for tap in (1, 2):
            total = total + by[tap] * shifted[slot, pl.ds(8 + BLOCK * b - tap, BLOCK), :]
        return total

    def slot_rows(d):
        return pl.ds(pl.multiple_of(d * (BLOCK + EDGES), 8), BLOCK + EDGES)

    def sums_copy(t):
        return pltpu.make_async_remote_copy(
            src_ref=sums_out.at[t], dst_ref=sums_in.at[slot_rows(me)], send_sem=sums_send.at[t], recv_sem=sums_recv.at[me],
            device_id={"ctx": t}, device_id_type=MESH)

    halfs = PER_CHUNK // 2

    def pair_at(q):
        return chunk_at(q // halfs), lax.rem(me // 2 + lax.rem(q, halfs), halfs)

    mask = group_mask(LANES)

    def values_pair(q):
        c, p = pair_at(q)
        for side in range(2):
            j = 2 * p + side
            t = c * PER_CHUNK + j
            for s in range(3):
                lane = pl.ds(pl.multiple_of(s * channels + t * LANES, LANES), LANES)
                rim_out[s * chunks + c, pl.ds(2 * j, 2), :] = last[:, lane].astype(F32)[BLOCK - 2:]
            lane = pl.ds(pl.multiple_of(t * LANES, LANES), LANES)
            at_key, at_value = 2 * side, 2 * side + 1
            shifted_rows(at_key, 1, c, j)
            shifted_rows(at_value, 2, c, j)
            by_key, by_value = stream_taps(1, t), stream_taps(2, t)
            direct = skip[0:1, lane]
            for b in range(blocks):
                at = pl.ds(b * BLOCK, BLOCK)
                inner = filtered(at_key, by_key, b) * filtered(at_value, by_value, b)
                loc[at, lane] = direct * inner
                u_high[at, lane], u_low[at, lane] = halves(inner)
            end = 6 + rows
            sums_out[t, pl.ds(BLOCK, 2)] = shifted[at_key, pl.ds(8, 2), :]
            sums_out[t, pl.ds(BLOCK + 2, 2)] = shifted[at_value, pl.ds(8, 2), :]
            sums_out[t, pl.ds(BLOCK + 4, 2)] = shifted[at_key, pl.ds(end, 2), :]
            sums_out[t, pl.ds(BLOCK + 6, 2)] = shifted[at_value, pl.ds(end, 2), :]

    def sums_pair(q):
        c, p = pair_at(q)
        pair = c * halfs + p
        lane = pl.ds(pl.multiple_of(pair * PAIR, PAIR), PAIR)
        high, low = u_high[:, lane], u_low[:, lane]
        by = backward[pair]
        every = jnp.dot(jnp.concatenate([by, by[:, :rows]], axis=1), jnp.concatenate([high, high, low], axis=0),
                        preferred_element_type=F32)
        own = lax.broadcasted_iota(jnp.int32, (BLOCK, LANES), 1) // BLOCK
        for side in range(2):
            total = jnp.zeros((BLOCK, LANES), F32)
            for g in range(LANES // BLOCK):
                at = (side * (LANES // BLOCK) + g) * BLOCK
                total = jnp.where(own == g, every[at:at + BLOCK, side * LANES:(side + 1) * LANES], total)
            sums_out[2 * pair + side, 0:BLOCK] = total

    def send_pair(q):
        c, p = pair_at(q)
        for side in range(2):
            t = c * PER_CHUNK + 2 * p + side

            @pl.when(t != me)
            def _():
                sums_copy(t).start()

    def chunk_wait(q):
        @pl.when(lax.rem(q, halfs) == 0)
        def _():
            c = chunk_at(q // halfs)
            stream_copy(1, c).wait()
            stream_copy(2, c).wait()
            stream_copy(0, c).start()

    pairs = tiles // 2
    greeted = pairs // 2
    chunk_wait(0)
    backward_pair(0)
    values_pair(0)

    @pl.loop(1, greeted)
    def _(q):
        chunk_wait(q)
        sums_pair(q - 1)
        backward_pair(q)
        values_pair(q)

    pl.semaphore_wait(barrier, count - 1)

    @pl.loop(0, greeted - 1)
    def _(q):
        send_pair(q)

    @pl.loop(greeted, pairs)
    def _(q):
        chunk_wait(q)
        sums_pair(q - 1)
        backward_pair(q)
        values_pair(q)
        send_pair(q - 1)

    sums_pair(pairs - 1)
    send_pair(pairs - 1)
    sums_in[slot_rows(me), :] = sums_out[me]

    rim_copy.start()

    @pl.loop(0, chunks)
    def _(k):
        stream_copy(0, chunk_at(k)).wait()

    pick = lax.broadcasted_iota(jnp.int32, (BLOCK, LANES), 1) // BLOCK
    groups = LANES // BLOCK

    def filters_stage(u, t):
        lane = pl.ds(pl.multiple_of(t * LANES, LANES), LANES)
        inside = lax.broadcasted_iota(jnp.int32, (BLOCK, LANES), 1) % BLOCK
        row = lax.broadcasted_iota(jnp.int32, (BLOCK, LANES), 0)
        r, a = picked(few_rates, t * groups, pick), picked(few_amps, t * groups, pick)
        own = row == inside
        r_own = jnp.sum(jnp.where(own, r, 0.0), axis=0, keepdims=True)
        a_own = jnp.sum(jnp.where(own, a, 0.0), axis=0, keepdims=True)
        out = a_own * jnp.exp(-r_own * (row.astype(F32) + 1.0))
        step = jnp.exp(-float(BLOCK) * r_own)
        near = []
        for b in range(blocks):
            high, low = halves(out)
            forward_high[pl.ds(b * BLOCK, BLOCK), lane] = high
            forward_low[pl.ds(b * BLOCK, BLOCK), lane] = low
            if b < 2:
                near.append((high, low))
            out = out * step
        by = stack_rows([(near[0][0], False), (near[1][0], False), (near[0][1], True), (near[1][1], True)])
        inside = inside.astype(F32)
        high, low = halves(jnp.exp(r * (inside + 1.0)))
        span = jnp.dot(by, jnp.concatenate([spread(mask, high), spread(mask, low)], axis=0), preferred_element_type=F32)
        span = span[:SPAN] + span[SPAN:]
        near = halves(jnp.where(row.astype(F32) >= inside, span[:BLOCK], 0.0))
        far = halves(span[BLOCK:])
        back = halves(jnp.exp(-r * (BLOCK - 1.0 - inside)))
        weights[u] = stack_rows([(far[0], False), (far[1], True), (near[0], False), (back[0], False),
                                 (near[1], True), (back[1], True)])

    def near_stage(u, t):
        lane = pl.ds(pl.multiple_of(t * LANES, LANES), LANES)
        step = jnp.exp(-float(BLOCK) * picked(few_rates, t * groups, pick))
        by = weights[u]

        def block_u(b):
            at = pl.ds(b * BLOCK, BLOCK)
            return u_high[at, lane], u_low[at, lane]

        products = []
        for quad in range(blocks // 4):
            products.append((
                jnp.dot(by, paired(mask, block_u(4 * quad), block_u(4 * quad + 2)), preferred_element_type=F32),
                jnp.dot(by[2 * BLOCK:], paired(mask, block_u(4 * quad + 1), block_u(4 * quad + 3)),
                        preferred_element_type=F32)))
        state = jnp.zeros((BLOCK, LANES), F32)
        for b in range(blocks):
            even, odd = products[b // 4]
            side = slice((b % 4 // 2) * LANES, (b % 4 // 2 + 1) * LANES)
            part = odd[:, side] if b % 2 else even[2 * BLOCK:, side]
            value = part[:BLOCK] + part[2 * BLOCK:3 * BLOCK]
            if b % 2:
                value = value + (even[:BLOCK, side] + even[BLOCK:2 * BLOCK, side])
            else:
                states[u, b // 2, 0], states[u, b // 2, 1] = halves(state)
            loc[pl.ds(b * BLOCK, BLOCK), lane] += value
            state = state * step + (part[BLOCK:2 * BLOCK] + part[3 * BLOCK:])

    def gate_stage(u, t):
        lane = pl.ds(pl.multiple_of(t * LANES, LANES), LANES)
        low = forward_low[0:SPAN, lane]
        by = stack_rows([(forward_high[0:SPAN, lane], False), (low, True)])
        products = [jnp.dot(by, paired(mask, (states[u, m, 0], states[u, m, 1]), (states[u, m + 1, 0], states[u, m + 1, 1])),
                            preferred_element_type=F32) for m in range(0, rows // SPAN, 2)]
        shifted_rows(u, 0, t // PER_CHUNK, lax.rem(t, PER_CHUNK))
        by_query = stream_taps(0, t)
        for b in range(blocks):
            at = pl.ds(b * BLOCK, BLOCK)
            value = products[b // 4][:, (b % 4 // 2) * LANES:(b % 4 // 2 + 1) * LANES]
            half = (b % 2) * BLOCK
            total = loc[at, lane] + (value[half:half + BLOCK] + value[SPAN + half:SPAN + half + BLOCK])
            if b == 0:
                first_rows[t] = total[:8]
            gate = filtered(u, by_query, b)
            query[at, lane] = gate
            loc[at, lane] = gate * total

    def stages(i, which):
        for stage, back in ((gate_stage, 2), (near_stage, 1), (filters_stage, 0)):
            if back in which:
                for u in range(UNROLL):
                    stage(u, (i - back) * UNROLL + u)

    steps = tiles // UNROLL
    answered = steps // 2
    stages(0, (0,))
    stages(1, (0, 1))

    @pl.loop(2, answered)
    def _(i):
        stages(i, (0, 1, 2))

    def sums_arrival(d):
        return pltpu.make_async_remote_copy(
            src_ref=sums_out.at[d], dst_ref=sums_in.at[slot_rows(d)], send_sem=sums_send.at[d], recv_sem=sums_recv.at[d],
            device_id={"ctx": d}, device_id_type=MESH)

    def back_copy(d):
        return pltpu.make_async_remote_copy(
            src_ref=back_out.at[d], dst_ref=back_in.at[me], send_sem=back_send.at[d], recv_sem=back_recv.at[me],
            device_id={"ctx": d}, device_id_type=MESH)

    def back_arrival(d):
        return pltpu.make_async_remote_copy(
            src_ref=back_out.at[d], dst_ref=back_in.at[d], send_sem=back_send.at[d], recv_sem=back_recv.at[d],
            device_id={"ctx": d}, device_id_type=MESH)

    @pl.loop(1, count)
    def _(i):
        sums_arrival(lax.rem(me + i, count)).wait_recv()

    r = picked(few_rates, me * groups, pick)
    device_decay = jnp.exp(-float(rows) * r)
    ahead = jnp.exp(r)
    further = ahead * ahead
    key_taps, value_taps = stream_taps(1, me), stream_taps(2, me)
    edge = [sums_in[pl.ds(BLOCK + i, count, stride=BLOCK + EDGES), :] for i in range(EDGES)]
    rim = [jnp.concatenate([jnp.zeros((1, LANES), F32), x[:-1]], axis=0) for x in edge[4:]]
    first, second = rim_effect(key_taps, value_taps, edge[:4], rim)
    state = jnp.zeros((BLOCK, LANES), F32)
    for d in range(count):
        state = state + (ahead * first[d:d + 1] + further * second[d:d + 1])
        back_out[d] = state
        state = state * device_decay + sums_in[d * (BLOCK + EDGES):d * (BLOCK + EDGES) + BLOCK, :]
    back_in[me] = back_out[me]

    @pl.loop(1, count)
    def _(i):
        back_copy(lax.rem(me + i, count)).start()

    @pl.loop(answered, steps)
    def _(i):
        stages(i, (0, 1, 2))

    stages(steps, (1, 2))
    stages(steps + 1, (2,))

    rim_copy.wait()
    has_rim = jnp.where(me > 0, 1.0, 0.0)

    @pl.loop(0, chunks, step=2)
    def _(two):
        for i in range(2 * PER_CHUNK):
            c, j = two + i // PER_CHUNK, i % PER_CHUNK
            t = c * PER_CHUNK + j
            lane = pl.ds(pl.multiple_of(t * LANES, LANES), LANES)
            rim = [rim_in[s * chunks + c, 2 * j:2 * j + 2, :] * has_rim for s in range(3)]
            edge = sums_out[t, pl.ds(BLOCK, 4)]
            first, second = rim_effect(
                stream_taps(1, t), stream_taps(2, t), [edge[i:i + 1] for i in range(4)],
                [rim[1][0:1], rim[1][1:2], rim[2][0:1], rim[2][1:2]])
            r, a = picked(few_rates, t * groups, pick), picked(few_amps, t * groups, pick)
            before = jnp.sum(a * jnp.exp(r), axis=0, keepdims=True)
            direct = skip[0:1, lane]
            by_query = stream_taps(0, t)
            total = first_rows[t]
            gate = query[0:8, lane]
            gates = (gate[0:1] + by_query[1] * rim[0][1:2] + by_query[2] * rim[0][0:1],
                     gate[1:2] + by_query[2] * rim[0][1:2])
            totals = (total[0:1] + direct * first - before * second, total[1:2] + direct * second)
            for i in range(2):
                query[i:i + 1, lane] = gates[i]
                loc[i:i + 1, lane] = gates[i] * totals[i]

    @pl.loop(1, count)
    def _(i):
        d = lax.rem(me + i, count)
        back_arrival(d).wait_recv()
        sums_arrival(d).wait_send()
        back_copy(d).wait_send()

    for t in range(tiles):
        incoming[:, t * LANES:(t + 1) * LANES] = back_in[t]


def last_kernel(loc, query, forward_high, forward_low, incoming, out, held, sems):
    channels = loc.shape[1]
    mask = group_mask(PAIR)
    copies = []
    for start in range(0, channels, WIDE):
        for first in range(start, start + WIDE, PAIR):
            lane = slice(first, first + PAIR)
            high, low = halves(incoming[:, lane])
            high, low = spread(mask, high), spread(mask, low)
            by_high, by_low = forward_high[:, lane], forward_low[:, lane]
            value = jnp.dot(jnp.concatenate([by_high, by_low, by_high], axis=1),
                            jnp.concatenate([high, high, low], axis=0), preferred_element_type=F32)
            held[:, lane] = loc[:, lane] + query[:, lane] * value
        lane = slice(start, start + WIDE)
        copies.append(pltpu.make_async_copy(held.at[:, lane], out.at[:, lane], sems.at[start // WIDE]))
        copies[-1].start()
    for copy in copies:
        copy.wait()


def body(count, streams, short_filter, rates, residues, skip):
    rows = streams.shape[0]
    channels = skip.shape[0]
    groups = rates.shape[0]
    tiles = channels // LANES
    chunks = tiles // PER_CHUNK
    vmem = pl.BlockSpec(memory_space=pltpu.VMEM)
    hbm = pl.BlockSpec(memory_space=pltpu.HBM)
    shapes = (
        ((rows, channels), F32),
        ((rows, channels), F32),
        ((rows, channels), BF16),
        ((rows, channels), BF16),
        ((BLOCK, channels), F32),
    )
    operands = (streams, short_filter, rates.T, residues.T, skip[None, :])
    operands = [pltpu.with_memory_space_constraint(x, pltpu.HBM) for x in operands]
    parts = pl.pallas_call(
        functools.partial(main_kernel, count),
        out_shape=tuple(pltpu.VMEM(shape, dtype) for shape, dtype in shapes),
        in_specs=[hbm] * 5,
        out_specs=(vmem,) * len(shapes),
        scratch_shapes=[
            pltpu.VMEM((3, chunks, rows, WIDE), BF16),
            pltpu.VMEM((BLOCK, 3 * channels), BF16),
            pltpu.VMEM(short_filter.shape, F32),
            pltpu.VMEM((1, channels), F32),
            pltpu.VMEM((BLOCK, groups), F32),
            pltpu.VMEM((BLOCK, groups), F32),
            pltpu.VMEM((tiles // 2, PAIR, 2 * rows), BF16),
            pltpu.VMEM((rows, channels), BF16),
            pltpu.VMEM((rows, channels), BF16),
            pltpu.VMEM((tiles, 8, LANES), F32),
            pltpu.VMEM((UNROLL, 6 * BLOCK, PAIR), BF16),
            pltpu.VMEM((UNROLL, rows // SPAN, 2, BLOCK, LANES), BF16),
            pltpu.VMEM((3 * chunks, 8, LANES), F32),
            pltpu.VMEM((3 * chunks, 8, LANES), F32),
            pltpu.VMEM((max(4, UNROLL), rows + 8, LANES), F32),
            pltpu.VMEM((count, BLOCK + EDGES, LANES), F32),
            pltpu.VMEM((count * (BLOCK + EDGES), LANES), F32),
            pltpu.VMEM((count, BLOCK, LANES), F32),
            pltpu.VMEM((count, BLOCK, LANES), F32),
            pltpu.SemaphoreType.DMA((3, chunks)),
            pltpu.SemaphoreType.DMA((5,)),
            pltpu.SemaphoreType.DMA((2,)),
            pltpu.SemaphoreType.DMA((count,)),
            pltpu.SemaphoreType.DMA((count,)),
            pltpu.SemaphoreType.DMA((count,)),
            pltpu.SemaphoreType.DMA((count,)),
        ],
        compiler_params=pltpu.CompilerParams(
            collective_id=0, has_side_effects=True, vmem_limit_bytes=24 << 20),
        name="local_part",
    )(*operands)
    parts = [pltpu.with_memory_space_constraint(part, pltpu.VMEM) for part in parts]
    return pl.pallas_call(
        last_kernel,
        out_shape=jax.ShapeDtypeStruct((rows, channels), F32),
        in_specs=[vmem] * len(parts),
        out_specs=hbm,
        scratch_shapes=[pltpu.VMEM((rows, channels), F32), pltpu.SemaphoreType.DMA((chunks,))],
        compiler_params=pltpu.CompilerParams(vmem_limit_bytes=16 << 20),
        name="carried_part",
    )(*parts)


def solution(mesh):
    count = mesh.shape["ctx"]
    in_specs = (P(("dp", "ctx"), None), P(), P(), P(), P())
    out_specs = P(("dp", "ctx"), None)
    return jax.shard_map(functools.partial(body, count), mesh=mesh, in_specs=in_specs, out_specs=out_specs,
                         check_vma=False)
```

```python
import functools

import jax
import jax.numpy as jnp
from jax import lax
from jax.experimental import pallas as pl
from jax.experimental.pallas import tpu as pltpu
from jax.sharding import PartitionSpec as P

F32 = jnp.float32
BF16 = jnp.bfloat16
LANES = 128
BLOCK = 16
SPAN = 2 * BLOCK
PER_CHUNK = 4
WIDE = PER_CHUNK * LANES
EDGES = 8
PAIR = 2 * LANES
UNROLL = 4
MESH = pl.DeviceIdType.MESH


def halves(x):
    high = x.astype(BF16)
    return high, (x - high.astype(F32)).astype(BF16)


def group_mask(lanes):
    row = lax.broadcasted_iota(jnp.int32, (lanes, lanes), 0) // BLOCK
    lane = lax.broadcasted_iota(jnp.int32, (lanes, lanes), 1) // BLOCK
    return row == lane


def spread(mask, x):
    return jnp.where(mask, jnp.concatenate([x] * (mask.shape[0] // BLOCK), axis=0), jnp.zeros((), BF16))


def paired(mask, first, second):
    left = jnp.concatenate([spread(mask, first[0]), spread(mask, first[1])], axis=0)
    right = jnp.concatenate([spread(mask, second[0]), spread(mask, second[1])], axis=0)
    return jnp.concatenate([left, right], axis=1)


def stack_rows(parts):
    rows = []
    for part, is_low in parts:
        other = jnp.zeros_like(part) if is_low else part
        rows.append(jnp.concatenate([part, other], axis=1))
    return jnp.concatenate(rows, axis=0)


def rim_effect(key_taps, value_taps, edge, rim):
    k0, k1, v0, v1 = edge
    kb, ka, vb, va = rim
    base_k, base_v = key_taps[0] * k0, value_taps[0] * v0
    more_k, more_v = key_taps[1] * ka + key_taps[2] * kb, value_taps[1] * va + value_taps[2] * vb
    first = more_k * base_v + (base_k + more_k) * more_v
    base_k, base_v = key_taps[0] * k1 + key_taps[1] * k0, value_taps[0] * v1 + value_taps[1] * v0
    more_k, more_v = key_taps[2] * ka, value_taps[2] * va
    second = more_k * base_v + (base_k + more_k) * more_v
    return first, second


def main_kernel(
    count, streams, taps_in, rates, residues, skip_in,
    loc, query, forward_high, forward_low, incoming,
    xs, last, taps, skip, few_rates, few_amps, backward, u_high, u_low, first_rows,
    weights, states, rim_out, rim_in, shifted, sums_out, sums_in, back_out, back_in,
    stream_sem, small_sem, rim_sems, sums_send, sums_recv, back_send, back_recv,
):
    rows, channels = loc.shape
    tiles = channels // LANES
    chunks = tiles // PER_CHUNK
    blocks = rows // BLOCK
    me = lax.axis_index("ctx")

    def stream_copy(s, c):
        return pltpu.make_async_copy(
            streams.at[:, pl.ds(pl.multiple_of(s * channels + c * WIDE, WIDE), WIDE)],
            xs.at[s, c], stream_sem.at[s, c])

    def chunk_at(k):
        return lax.rem(me // PER_CHUNK + 1 + k, chunks)

    small = [pltpu.make_async_copy(a, b, small_sem.at[i]) for i, (a, b) in enumerate((
        (rates, few_rates), (residues, few_amps), (taps_in, taps), (skip_in, skip),
        (streams.at[pl.ds(rows - BLOCK, BLOCK), :], last)))]
    for copy in small:
        copy.start()

    @pl.loop(0, chunks)
    def _(k):
        c = chunk_at(k)
        stream_copy(1, c).start()
        stream_copy(2, c).start()

    barrier = pltpu.get_barrier_semaphore()

    @pl.loop(1, count)
    def _(i):
        pl.semaphore_signal(barrier, inc=1, device_id={"ctx": lax.rem(me + i, count)}, device_id_type=MESH)


    small[0].wait()
    small[1].wait()
    few = few_rates[...]
    few_amps[...] = few_amps[...] * (few * (1.0 - few / 2 * (1.0 - few / 3 * (1.0 - few / 4 * (
        1.0 - few / 5 * (1.0 - few / 6))))))

    def picked(ref, group, index):
        part = pl.ds(pl.multiple_of(group // LANES * LANES, LANES), LANES)
        return jnp.take_along_axis(ref[:, part], index + lax.rem(group, LANES), axis=1, mode="promise_in_bounds")

    def backward_pair(q):
        c, p = pair_at(q)
        t = c * halfs + p
        zero = jnp.zeros((BLOCK, LANES), jnp.int32)
        gap = LANES - 1.0 - lax.broadcasted_iota(jnp.int32, (BLOCK, LANES), 1).astype(F32)
        for g in range(PAIR // BLOCK):
            r = picked(few_rates, t * (PAIR // BLOCK) + g, zero)
            piece = jnp.exp(-r * gap)
            step = jnp.exp(-float(LANES) * r)
            pieces = [piece]
            for _ in range(rows // LANES - 1):
                pieces.append(pieces[-1] * step)
            for i, piece in enumerate(pieces[::-1]):
                high, low = halves(piece)
                backward[t, pl.ds(g * BLOCK, BLOCK), i * LANES:(i + 1) * LANES] = high
                backward[t, pl.ds(g * BLOCK, BLOCK), rows + i * LANES:rows + (i + 1) * LANES] = low

    for copy in small[2:]:
        copy.wait()

    rim_copy = pltpu.make_async_remote_copy(
        src_ref=rim_out, dst_ref=rim_in, send_sem=rim_sems.at[0], recv_sem=rim_sems.at[1],
        device_id={"ctx": lax.rem(me + 1, count)}, device_id_type=MESH)

    def shifted_rows(slot, s, c, j):
        lane = pl.ds(pl.multiple_of(j * LANES, LANES), LANES)
        shifted[slot, pl.ds(6, 2), :] = jnp.zeros((2, LANES), F32)
        for b in range(blocks):
            shifted[slot, pl.ds(8 + BLOCK * b, BLOCK), :] = xs[s, c, pl.ds(BLOCK * b, BLOCK), lane].astype(F32)

    def stream_taps(s, t):
        lane = pl.ds(pl.multiple_of(s * channels + t * LANES, LANES), LANES)
        return [taps[tap:tap + 1, lane] for tap in range(3)]

    def filtered(slot, by, b):
        total = by[0] * shifted[slot, pl.ds(8 + BLOCK * b, BLOCK), :]
        for tap in (1, 2):
            total = total + by[tap] * shifted[slot, pl.ds(8 + BLOCK * b - tap, BLOCK), :]
        return total

    def slot_rows(d):
        return pl.ds(pl.multiple_of(d * (BLOCK + EDGES), 8), BLOCK + EDGES)

    def sums_copy(t):
        return pltpu.make_async_remote_copy(
            src_ref=sums_out.at[t], dst_ref=sums_in.at[slot_rows(me)], send_sem=sums_send.at[t], recv_sem=sums_recv.at[me],
            device_id={"ctx": t}, device_id_type=MESH)

    halfs = PER_CHUNK // 2

    def pair_at(q):
        return chunk_at(q // halfs), lax.rem(me // 2 + lax.rem(q, halfs), halfs)

    mask = group_mask(LANES)

    def values_pair(q):
        c, p = pair_at(q)
        for side in range(2):
            j = 2 * p + side
            t = c * PER_CHUNK + j
            for s in range(3):
                lane = pl.ds(pl.multiple_of(s * channels + t * LANES, LANES), LANES)
                rim_out[s * chunks + c, pl.ds(2 * j, 2), :] = last[:, lane].astype(F32)[BLOCK - 2:]
            lane = pl.ds(pl.multiple_of(t * LANES, LANES), LANES)
            at_key, at_value = 2 * side, 2 * side + 1
            shifted_rows(at_key, 1, c, j)
            shifted_rows(at_value, 2, c, j)
            by_key, by_value = stream_taps(1, t), stream_taps(2, t)
            direct = skip[0:1, lane]
            for b in range(blocks):
                at = pl.ds(b * BLOCK, BLOCK)
                inner = filtered(at_key, by_key, b) * filtered(at_value, by_value, b)
                loc[at, lane] = direct * inner
                u_high[at, lane], u_low[at, lane] = halves(inner)
            end = 6 + rows
            sums_out[t, pl.ds(BLOCK, 2)] = shifted[at_key, pl.ds(8, 2), :]
            sums_out[t, pl.ds(BLOCK + 2, 2)] = shifted[at_value, pl.ds(8, 2), :]
            sums_out[t, pl.ds(BLOCK + 4, 2)] = shifted[at_key, pl.ds(end, 2), :]
            sums_out[t, pl.ds(BLOCK + 6, 2)] = shifted[at_value, pl.ds(end, 2), :]

    def sums_pair(q):
        c, p = pair_at(q)
        pair = c * halfs + p
        lane = pl.ds(pl.multiple_of(pair * PAIR, PAIR), PAIR)
        high, low = u_high[:, lane], u_low[:, lane]
        by = backward[pair]
        every = jnp.dot(jnp.concatenate([by, by[:, :rows]], axis=1), jnp.concatenate([high, high, low], axis=0),
                        preferred_element_type=F32)
        own = lax.broadcasted_iota(jnp.int32, (BLOCK, LANES), 1) // BLOCK
        for side in range(2):
            total = jnp.zeros((BLOCK, LANES), F32)
            for g in range(LANES // BLOCK):
                at = (side * (LANES // BLOCK) + g) * BLOCK
                total = jnp.where(own == g, every[at:at + BLOCK, side * LANES:(side + 1) * LANES], total)
            sums_out[2 * pair + side, 0:BLOCK] = total

    def send_pair(q):
        c, p = pair_at(q)
        for side in range(2):
            t = c * PER_CHUNK + 2 * p + side

            @pl.when(t != me)
            def _():
                sums_copy(t).start()

    def chunk_wait(q):
        @pl.when(lax.rem(q, halfs) == 0)
        def _():
            c = chunk_at(q // halfs)
            stream_copy(1, c).wait()
            stream_copy(2, c).wait()
            stream_copy(0, c).start()

    pairs = tiles // 2
    greeted = pairs // 2
    chunk_wait(0)
    backward_pair(0)
    values_pair(0)

    @pl.loop(1, greeted)
    def _(q):
        chunk_wait(q)
        sums_pair(q - 1)
        backward_pair(q)
        values_pair(q)

    pl.semaphore_wait(barrier, count - 1)

    @pl.loop(0, greeted - 1)
    def _(q):
        send_pair(q)

    @pl.loop(greeted, pairs)
    def _(q):
        chunk_wait(q)
        sums_pair(q - 1)
        backward_pair(q)
        values_pair(q)
        send_pair(q - 1)

    sums_pair(pairs - 1)
    send_pair(pairs - 1)
    sums_in[slot_rows(me), :] = sums_out[me]

    rim_copy.start()

    @pl.loop(0, chunks)
    def _(k):
        stream_copy(0, chunk_at(k)).wait()

    pick = lax.broadcasted_iota(jnp.int32, (BLOCK, LANES), 1) // BLOCK
    groups = LANES // BLOCK

    def filters_stage(u, t):
        lane = pl.ds(pl.multiple_of(t * LANES, LANES), LANES)
        inside = lax.broadcasted_iota(jnp.int32, (BLOCK, LANES), 1) % BLOCK
        row = lax.broadcasted_iota(jnp.int32, (BLOCK, LANES), 0)
        r, a = picked(few_rates, t * groups, pick), picked(few_amps, t * groups, pick)
        own = row == inside
        r_own = jnp.sum(jnp.where(own, r, 0.0), axis=0, keepdims=True)
        a_own = jnp.sum(jnp.where(own, a, 0.0), axis=0, keepdims=True)
        out = a_own * jnp.exp(-r_own * (row.astype(F32) + 1.0))
        step = jnp.exp(-float(BLOCK) * r_own)
        near = []
        for b in range(blocks):
            high, low = halves(out)
            forward_high[pl.ds(b * BLOCK, BLOCK), lane] = high
            forward_low[pl.ds(b * BLOCK, BLOCK), lane] = low
            if b < 2:
                near.append((high, low))
            out = out * step
        by = stack_rows([(near[0][0], False), (near[1][0], False), (near[0][1], True), (near[1][1], True)])
        inside = inside.astype(F32)
        high, low = halves(jnp.exp(r * (inside + 1.0)))
        span = jnp.dot(by, jnp.concatenate([spread(mask, high), spread(mask, low)], axis=0), preferred_element_type=F32)
        span = span[:SPAN] + span[SPAN:]
        near = halves(jnp.where(row.astype(F32) >= inside, span[:BLOCK], 0.0))
        far = halves(span[BLOCK:])
        back = halves(jnp.exp(-r * (BLOCK - 1.0 - inside)))
        weights[u] = stack_rows([(far[0], False), (far[1], True), (near[0], False), (back[0], False),
                                 (near[1], True), (back[1], True)])

    def near_stage(u, t):
        lane = pl.ds(pl.multiple_of(t * LANES, LANES), LANES)
        step = jnp.exp(-float(BLOCK) * picked(few_rates, t * groups, pick))
        by = weights[u]

        def block_u(b):
            at = pl.ds(b * BLOCK, BLOCK)
            return u_high[at, lane], u_low[at, lane]

        products = []
        for quad in range(blocks // 4):
            products.append((
                jnp.dot(by, paired(mask, block_u(4 * quad), block_u(4 * quad + 2)), preferred_element_type=F32),
                jnp.dot(by[2 * BLOCK:], paired(mask, block_u(4 * quad + 1), block_u(4 * quad + 3)),
                        preferred_element_type=F32)))
        state = jnp.zeros((BLOCK, LANES), F32)
        for b in range(blocks):
            even, odd = products[b // 4]
            side = slice((b % 4 // 2) * LANES, (b % 4 // 2 + 1) * LANES)
            part = odd[:, side] if b % 2 else even[2 * BLOCK:, side]
            value = part[:BLOCK] + part[2 * BLOCK:3 * BLOCK]
            if b % 2:
                value = value + (even[:BLOCK, side] + even[BLOCK:2 * BLOCK, side])
            else:
                states[u, b // 2, 0], states[u, b // 2, 1] = halves(state)
            loc[pl.ds(b * BLOCK, BLOCK), lane] += value
            state = state * step + (part[BLOCK:2 * BLOCK] + part[3 * BLOCK:])

    def gate_stage(u, t):
        lane = pl.ds(pl.multiple_of(t * LANES, LANES), LANES)
        low = forward_low[0:SPAN, lane]
        by = stack_rows([(forward_high[0:SPAN, lane], False), (low, True)])
        products = [jnp.dot(by, paired(mask, (states[u, m, 0], states[u, m, 1]), (states[u, m + 1, 0], states[u, m + 1, 1])),
                            preferred_element_type=F32) for m in range(0, rows // SPAN, 2)]
        shifted_rows(u, 0, t // PER_CHUNK, lax.rem(t, PER_CHUNK))
        by_query = stream_taps(0, t)
        for b in range(blocks):
            at = pl.ds(b * BLOCK, BLOCK)
            value = products[b // 4][:, (b % 4 // 2) * LANES:(b % 4 // 2 + 1) * LANES]
            half = (b % 2) * BLOCK
            total = loc[at, lane] + (value[half:half + BLOCK] + value[SPAN + half:SPAN + half + BLOCK])
            if b == 0:
                first_rows[t] = total[:8]
            gate = filtered(u, by_query, b)
            query[at, lane] = gate
            loc[at, lane] = gate * total

    def stages(i, which):
        for u in range(UNROLL):
            for stage, back in ((gate_stage, 2), (near_stage, 1), (filters_stage, 0)):
                if back in which:
                    stage(u, (i - back) * UNROLL + u)

    steps = tiles // UNROLL
    answered = steps // 2
    stages(0, (0,))
    stages(1, (0, 1))

    @pl.loop(2, answered)
    def _(i):
        stages(i, (0, 1, 2))

    def sums_arrival(d):
        return pltpu.make_async_remote_copy(
            src_ref=sums_out.at[d], dst_ref=sums_in.at[slot_rows(d)], send_sem=sums_send.at[d], recv_sem=sums_recv.at[d],
            device_id={"ctx": d}, device_id_type=MESH)

    def back_copy(d):
        return pltpu.make_async_remote_copy(
            src_ref=back_out.at[d], dst_ref=back_in.at[me], send_sem=back_send.at[d], recv_sem=back_recv.at[me],
            device_id={"ctx": d}, device_id_type=MESH)

    def back_arrival(d):
        return pltpu.make_async_remote_copy(
            src_ref=back_out.at[d], dst_ref=back_in.at[d], send_sem=back_send.at[d], recv_sem=back_recv.at[d],
            device_id={"ctx": d}, device_id_type=MESH)

    @pl.loop(1, count)
    def _(i):
        sums_arrival(lax.rem(me + i, count)).wait_recv()

    r = picked(few_rates, me * groups, pick)
    device_decay = jnp.exp(-float(rows) * r)
    ahead = jnp.exp(r)
    further = ahead * ahead
    key_taps, value_taps = stream_taps(1, me), stream_taps(2, me)
    edge = [sums_in[pl.ds(BLOCK + i, count, stride=BLOCK + EDGES), :] for i in range(EDGES)]
    rim = [jnp.concatenate([jnp.zeros((1, LANES), F32), x[:-1]], axis=0) for x in edge[4:]]
    first, second = rim_effect(key_taps, value_taps, edge[:4], rim)
    state = jnp.zeros((BLOCK, LANES), F32)
    for d in range(count):
        state = state + (ahead * first[d:d + 1] + further * second[d:d + 1])
        back_out[d] = state
        state = state * device_decay + sums_in[d * (BLOCK + EDGES):d * (BLOCK + EDGES) + BLOCK, :]
    back_in[me] = back_out[me]

    @pl.loop(1, count)
    def _(i):
        back_copy(lax.rem(me + i, count)).start()

    @pl.loop(answered, steps)
    def _(i):
        stages(i, (0, 1, 2))

    stages(steps, (1, 2))
    stages(steps + 1, (2,))

    rim_copy.wait()
    has_rim = jnp.where(me > 0, 1.0, 0.0)

    @pl.loop(0, chunks, step=chunks)
    def _(two):
        for i in range(chunks * PER_CHUNK):
            c, j = two + i // PER_CHUNK, i % PER_CHUNK
            t = c * PER_CHUNK + j
            lane = pl.ds(pl.multiple_of(t * LANES, LANES), LANES)
            rim = [rim_in[s * chunks + c, 2 * j:2 * j + 2, :] * has_rim for s in range(3)]
            edge = sums_out[t, pl.ds(BLOCK, 4)]
            first, second = rim_effect(
                stream_taps(1, t), stream_taps(2, t), [edge[i:i + 1] for i in range(4)],
                [rim[1][0:1], rim[1][1:2], rim[2][0:1], rim[2][1:2]])
            r, a = picked(few_rates, t * groups, pick), picked(few_amps, t * groups, pick)
            before = jnp.sum(a * jnp.exp(r), axis=0, keepdims=True)
            direct = skip[0:1, lane]
            by_query = stream_taps(0, t)
            total = first_rows[t]
            gate = query[0:8, lane]
            gates = (gate[0:1] + by_query[1] * rim[0][1:2] + by_query[2] * rim[0][0:1],
                     gate[1:2] + by_query[2] * rim[0][1:2])
            totals = (total[0:1] + direct * first - before * second, total[1:2] + direct * second)
            for i in range(2):
                query[i:i + 1, lane] = gates[i]
                loc[i:i + 1, lane] = gates[i] * totals[i]

    @pl.loop(1, count)
    def _(i):
        d = lax.rem(me + i, count)
        back_arrival(d).wait_recv()
        sums_arrival(d).wait_send()
        back_copy(d).wait_send()

    for t in range(tiles):
        incoming[:, t * LANES:(t + 1) * LANES] = back_in[t]


def last_kernel(loc, query, forward_high, forward_low, incoming, out, held, sems):
    channels = loc.shape[1]
    mask = group_mask(PAIR)
    copies = []
    for start in range(0, channels, WIDE):
        for first in range(start, start + WIDE, PAIR):
            lane = slice(first, first + PAIR)
            high, low = halves(incoming[:, lane])
            high, low = spread(mask, high), spread(mask, low)
            by_high, by_low = forward_high[:, lane], forward_low[:, lane]
            value = jnp.dot(jnp.concatenate([by_high, by_low, by_high], axis=1),
                            jnp.concatenate([high, high, low], axis=0), preferred_element_type=F32)
            held[:, lane] = loc[:, lane] + query[:, lane] * value
        lane = slice(start, start + WIDE)
        copies.append(pltpu.make_async_copy(held.at[:, lane], out.at[:, lane], sems.at[start // WIDE]))
        copies[-1].start()
    for copy in copies:
        copy.wait()


def body(count, streams, short_filter, rates, residues, skip):
    rows = streams.shape[0]
    channels = skip.shape[0]
    groups = rates.shape[0]
    tiles = channels // LANES
    chunks = tiles // PER_CHUNK
    vmem = pl.BlockSpec(memory_space=pltpu.VMEM)
    hbm = pl.BlockSpec(memory_space=pltpu.HBM)
    shapes = (
        ((rows, channels), F32),
        ((rows, channels), F32),
        ((rows, channels), BF16),
        ((rows, channels), BF16),
        ((BLOCK, channels), F32),
    )
    operands = (streams, short_filter, rates.T, residues.T, skip[None, :])
    operands = [pltpu.with_memory_space_constraint(x, pltpu.HBM) for x in operands]
    parts = pl.pallas_call(
        functools.partial(main_kernel, count),
        out_shape=tuple(pltpu.VMEM(shape, dtype) for shape, dtype in shapes),
        in_specs=[hbm] * 5,
        out_specs=(vmem,) * len(shapes),
        scratch_shapes=[
            pltpu.VMEM((3, chunks, rows, WIDE), BF16),
            pltpu.VMEM((BLOCK, 3 * channels), BF16),
            pltpu.VMEM(short_filter.shape, F32),
            pltpu.VMEM((1, channels), F32),
            pltpu.VMEM((BLOCK, groups), F32),
            pltpu.VMEM((BLOCK, groups), F32),
            pltpu.VMEM((tiles // 2, PAIR, 2 * rows), BF16),
            pltpu.VMEM((rows, channels), BF16),
            pltpu.VMEM((rows, channels), BF16),
            pltpu.VMEM((tiles, 8, LANES), F32),
            pltpu.VMEM((UNROLL, 6 * BLOCK, PAIR), BF16),
            pltpu.VMEM((UNROLL, rows // SPAN, 2, BLOCK, LANES), BF16),
            pltpu.VMEM((3 * chunks, 8, LANES), F32),
            pltpu.VMEM((3 * chunks, 8, LANES), F32),
            pltpu.VMEM((max(4, UNROLL), rows + 8, LANES), F32),
            pltpu.VMEM((count, BLOCK + EDGES, LANES), F32),
            pltpu.VMEM((count * (BLOCK + EDGES), LANES), F32),
            pltpu.VMEM((count, BLOCK, LANES), F32),
            pltpu.VMEM((count, BLOCK, LANES), F32),
            pltpu.SemaphoreType.DMA((3, chunks)),
            pltpu.SemaphoreType.DMA((5,)),
            pltpu.SemaphoreType.DMA((2,)),
            pltpu.SemaphoreType.DMA((count,)),
            pltpu.SemaphoreType.DMA((count,)),
            pltpu.SemaphoreType.DMA((count,)),
            pltpu.SemaphoreType.DMA((count,)),
        ],
        compiler_params=pltpu.CompilerParams(
            collective_id=0, has_side_effects=True, vmem_limit_bytes=24 << 20),
        name="local_part",
    )(*operands)
    parts = [pltpu.with_memory_space_constraint(part, pltpu.VMEM) for part in parts]
    return pl.pallas_call(
        last_kernel,
        out_shape=jax.ShapeDtypeStruct((rows, channels), F32),
        in_specs=[vmem] * len(parts),
        out_specs=hbm,
        scratch_shapes=[pltpu.VMEM((rows, channels), F32), pltpu.SemaphoreType.DMA((chunks,))],
        compiler_params=pltpu.CompilerParams(vmem_limit_bytes=16 << 20),
        name="carried_part",
    )(*parts)


def solution(mesh):
    count = mesh.shape["ctx"]
    in_specs = (P(("dp", "ctx"), None), P(), P(), P(), P())
    out_specs = P(("dp", "ctx"), None)
    return jax.shard_map(functools.partial(body, count), mesh=mesh, in_specs=in_specs, out_specs=out_specs,
                         check_vma=False)
```
